32 devices in a mesh: groups: 2 (over x), row: 16 (over z, y, core).
Axes of the slice: x: 2, y: 2, z: 4, core: 2. Of those that a mesh axis runs over, the one named last changes fastest.
Arguments:
- density: bfloat16 [512, 7, 128, 128], P(('groups', 'row')), parts along dimension 0, may hold values from -0.625 to 0.625
- block_cols: int32 [512, 7], P(('groups', 'row')), parts along dimension 0, may hold values from -1 to 255, as said below
Outputs:
- transposed: bfloat16 [512, 7, 128, 128], P(('groups', 'row')), parts along dimension 0
The draws below stay inside these ranges and needn't reach their ends.
There are 2 independent parts, one for each index of `groups`. The reference program is written for one: setup_inputs(seed, part) draws one part's arguments, and reference() takes and returns one part's arrays. A program takes and returns all parts, laid end to end along the dimension named above; each array names one. Nothing has to cross between parts.
Inputs may be any that keep to these rules, and one draw needn't show every extreme that they name: `block_cols`: block row i stands for the block at (i % 8, (i // 8) % 8, i // 64) of a grid of blocks. Its slots list, in this order, the columns i - 64, i - 8, i - 1, i, i + 1, i + 8, i + 64; slot 3 always holds i, and a neighbour slot holds -1 where that neighbour lies outside the grid or its pair is not kept. The pattern is symmetric: j is listed in row i exactly when i is listed in row j. Some row uses all 7 slots.
All inputs are finite; a program needn't handle non-finite values.
Results may differ from the reference program's by a relative error of at most 0.0051.
Values may be sent and summed in bfloat16 or wider, within the bound.
No kernel may reach another device: no remote copies, remote signals or barrier semaphores. Data moves between devices by JAX's collectives and lax.ppermute only.
A program may use at most 128 MiB of HBM per device.

```python
import jax
import jax.numpy as jnp
from jax import lax

BS = 128
K = 7
GX = 8
GY = 8
PLANE = 64
NB = 256


def draw_block_cols(key, part):
    key = jax.random.fold_in(key, 11)
    key_keep, key_ax, key_ay, key_az = jax.random.split(key, 4)
    row_ids = jnp.arange(NB, dtype=jnp.int32)[:, None]
    strides = jnp.array([1, GX, PLANE], dtype=jnp.int32)[None, :]
    coord_x = row_ids % GX
    coord_y = row_ids // GX % GY
    inside_up = jnp.concatenate([coord_x < GX - 1, coord_y < GY - 1, row_ids + PLANE < NB], axis=1)
    keep_edge = jax.random.randint(key_keep, (NB, 3), 0, 4) > 0
    anchor_x = jax.random.randint(key_ax, (), 1, GX - 1)
    anchor_y = jax.random.randint(key_ay, (), 1, GY - 1)
    anchor_z = jax.random.randint(key_az, (), 1, NB // PLANE - 1)
    anchor = (anchor_z * PLANE + anchor_y * GX + anchor_x).astype(jnp.int32)
    upper_cols = row_ids + strides
    kept_up = inside_up & (keep_edge | (row_ids == anchor) | (upper_cols == anchor))
    lower_cols = row_ids - strides
    slot_ids = jnp.arange(3, dtype=jnp.int32)[None, :]
    kept_down = (lower_cols >= 0) & kept_up[jnp.clip(lower_cols, 0, NB - 1), slot_ids]
    up_listed = jnp.where(kept_up, upper_cols, -1)
    down_listed = jnp.where(kept_down, lower_cols, -1)
    return jnp.concatenate([down_listed[:, ::-1], row_ids, up_listed], axis=1).astype(jnp.int32)


def shard_levels(own_key, extent, pieces, low, top_value):
    gain, own = 1.0, jax.random.fold_in(own_key, 6)
    for axis_at, shards_of in pieces:
        draws = jnp.exp(jax.random.uniform(jax.random.fold_in(own, axis_at), (shards_of,), jnp.float32, low / len(pieces), top_value / len(pieces)))
        gain = gain * jnp.repeat(draws, extent[axis_at] // shards_of).reshape([-1 if axis == axis_at else 1 for axis in range(len(extent))])
    return gain


def gaussian(key, dims, scale, most, cuts=(), kind=jnp.bfloat16):
    drawn = scale * jax.random.normal(key, dims, jnp.float32)
    if cuts:
        drawn = drawn * shard_levels(key, dims, cuts, -0.22, 0.18)
    return jnp.clip(drawn, -most, most).astype(kind)


def setup_inputs(seed: int = 0, part: int = 0) -> dict:
    keys = jax.random.split(jax.random.key(seed), 3)
    part_splits = jax.random.split(jax.random.fold_in(keys[2], part), 3)
    return {
        "density": gaussian(part_splits[0], (NB, K, BS, BS), 0.1, 0.625, ((0, 16),)),
        "block_cols": draw_block_cols(jax.random.fold_in(jax.random.fold_in(keys[2], part), 71), part),
    }


def row_product(left_blocks, row_cols, window_blocks, window_cols, locate):
    window_rows = locate(row_cols)
    rows_b = window_blocks[window_rows]
    rows_c = window_cols[window_rows]
    matched = (rows_c[:, :, None] == row_cols[None, None, :]) & (row_cols[None, None, :] >= 0)
    selector = matched.astype(jnp.float32)
    picked = jnp.einsum("abc,abmn->acmn", selector, rows_b.astype(jnp.float32)).astype(jnp.bfloat16)
    in_use = row_cols >= 0
    left_used = jnp.where(in_use[:, None, None], left_blocks, jnp.zeros_like(left_blocks))
    return jnp.einsum("arm,acmn->crn", left_used.astype(jnp.float32), picked.astype(jnp.float32))


def row_transpose(row_cols, column_id, window_blocks, window_cols, locate):
    window_rows = locate(row_cols)
    rows_b = window_blocks[window_rows]
    matched = (window_cols[window_rows] == column_id) & (row_cols[:, None] >= 0)
    selector = matched.astype(jnp.float32)
    return jnp.einsum("cb,cbmn->cnm", selector, rows_b.astype(jnp.float32)).astype(jnp.bfloat16)


def reference(density, block_cols):
    def locate(cols):
        return jnp.clip(cols, 0, NB - 1).astype(jnp.int32)

    def square_row(entry_pair):
        return row_product(entry_pair[0], entry_pair[1], density, block_cols, locate).astype(jnp.bfloat16)

    square = lax.map(square_row, (density, block_cols))

    def cube_row(entry_pair):
        return row_product(entry_pair[0], entry_pair[1], density, block_cols, locate)

    cube_part = lax.map(cube_row, (square, block_cols))
    purified = (3.0 * square.astype(jnp.float32) - 2.0 * cube_part).astype(jnp.bfloat16)
    column_ids = jnp.arange(NB, dtype=jnp.int32)

    def flip_row(entry_pair):
        return row_transpose(entry_pair[0], entry_pair[1], purified, block_cols, locate)

    return lax.map(flip_row, (block_cols, column_ids))
```

```python
import jax
import jax.numpy as jnp
from jax import lax
from jax.experimental import pallas as pl
from jax.experimental.pallas import tpu as pltpu
from jax.sharding import PartitionSpec as P

K = 7
GX = 8
PLANE = 64
CENTER = 3
BF16 = jnp.bfloat16
F32 = jnp.float32
VMEM_LIMIT = 48 * 1024 * 1024


def matching(value, parity, distance, period):
    count = lax.axis_size("row")
    pairs = []
    for source in range(count):
        place = source % period // distance
        step = distance if place % 2 == parity else -distance
        target = source + step
        if 0 <= target < count and target // period == source // period:
            pairs.append((source, target))
    return lax.ppermute(value, "row", pairs)


def dot(a, b):
    return jnp.dot(a, b, preferred_element_type=F32)


def masked(flag, block):
    return jnp.where(flag, block, jnp.zeros_like(block))


def rows_of(block_count, body, unroll=1):
    def step(i, carry):
        body(i)
        return carry

    lax.fori_loop(0, block_count, step, 0, unroll=unroll)


def local_edges(rows):
    edges = [(2, 1, 0, rows, -1), (4, 2, 0, rows, 1)]
    if rows > GX:
        edges += [(1, 0, GX, rows - GX, -GX), (5, 3, 0, rows - GX, GX)]
    return edges


def flip_diag_kernel(blocks, flipped):
    rows_of(flipped.shape[0], lambda j: flipped.__setitem__(j, blocks[j, CENTER].T), unroll=2)


def local_kernel(cols, blocks, diag_t, left_t, square_t, cube_t):
    rows = blocks.shape[0]
    for slot, place, first, count, step in local_edges(rows):

        def one(e, slot=slot, place=place, first=first, step=step):
            j = first + e
            k = jnp.clip(j + step, 0, rows - 1)
            x_t = masked(cols[j, slot] >= 0, blocks[k, K - 1 - slot]).T
            left_t[j, place] = x_t
            lhs = jnp.concatenate([diag_t[j], x_t], axis=1)
            rhs = jnp.concatenate([x_t, diag_t[k]], axis=0)
            square_t[j, place] = dot(lhs, rhs).astype(BF16)

        rows_of(count, one, unroll=2)
    lines = rows // GX
    for line in range(lines):

        def diag(x, line=line):
            j = line * GX + x
            lhs, rhs = [], []
            for slot, place, first, count, step in local_edges(rows):
                if first <= line * GX < first + count:
                    k = jnp.clip(j + step, 0, rows - 1)
                    lhs.append(left_t[j, place])
                    rhs.append(square_t[k, 3 - place])
            cube_t[j] = dot(jnp.concatenate(lhs, axis=1), jnp.concatenate(rhs, axis=0))

        rows_of(GX, diag, unroll=2)


def diag_square_kernel(cols, where, blocks, far_a, far_b, near_a, near_b, square_t, total):
    rows = blocks.shape[0]
    lines = rows // GX
    for line in range(lines):

        def local(x, line=line):
            j = line * GX + x
            lhs, rhs = [blocks[j, CENTER]], [blocks[j, CENTER]]
            for slot, place, first, count, step in local_edges(rows):
                if first <= line * GX < first + count:
                    k = jnp.clip(j + step, 0, rows - 1)
                    lhs.append(masked(cols[j, slot] >= 0, blocks[j, slot]))
                    rhs.append(blocks[k, K - 1 - slot])
            for far, at in ((far_a, 0), (far_b, 1)):
                lhs.append(masked(cols[j, where[at]] >= 0, blocks[j, where[at]]))
                rhs.append(far[j])
            total[j] = dot(jnp.concatenate(lhs, axis=1), jnp.concatenate(rhs, axis=0))

        rows_of(GX, local, unroll=2)
    for near, at in ((near_a, 2), (near_b, 4)):

        def edge(e, near=near, at=at):
            j = where[at + 1] + e
            left = masked(cols[j, where[at]] >= 0, blocks[j, where[at]])
            total[j] += dot(left, near[e])

        rows_of(GX, edge, unroll=2)
    rows_of(rows, lambda j: square_t.__setitem__(j, total[j].astype(BF16).T), unroll=2)


def remote_edge(flag, own, other, diag_own, diag_other):
    x_t = masked(flag, other).T
    y_t = masked(flag, own).T
    to_own = dot(jnp.concatenate([diag_own, x_t], axis=1), jnp.concatenate([x_t, diag_other], axis=0)).astype(BF16)
    to_other = dot(jnp.concatenate([diag_other, y_t], axis=1), jnp.concatenate([y_t, diag_own], axis=0)).astype(BF16)
    return x_t, to_own, dot(x_t, to_other)


def finish(diag_own, x_t, square, diag_square_other):
    cube = dot(jnp.concatenate([diag_own, x_t], axis=1), jnp.concatenate([square, diag_square_other], axis=0))
    return (3.0 * square.astype(F32) - 2.0 * cube).astype(BF16)


def near_kernel(
    cols, where, blocks, diag_t, left_t, square_t, cube_in, diag_square_t, near_a, near_b,
    out, near_left, near_square, cube_t, local_out, sem,
):
    rows = blocks.shape[0]
    for slot, place, first, count, step in local_edges(rows):

        def one(e, place=place, first=first, step=step):
            j = first + e
            k = jnp.clip(j + step, 0, rows - 1)
            local_out[place, j] = finish(diag_t[j], left_t[j, place], square_t[j, place], diag_square_t[k])

        rows_of(count, one, unroll=2)
        pltpu.make_async_copy(
            local_out.at[place, pl.ds(first, count)], out.at[pl.ds(first, count), slot], sem.at[place]
        ).start()
    rows_of(rows, lambda j: cube_t.__setitem__(j, cube_in[j]), unroll=2)
    for near, at, side in ((near_a, 2, 0), (near_b, 4, 1)):

        def edge(e, near=near, at=at, side=side):
            j = where[at + 1] + e
            x_t, square, cube = remote_edge(
                cols[j, where[at]] >= 0, blocks[j, where[at]], near[e], diag_t[j], near[GX + e]
            )
            near_left[side, e] = x_t
            near_square[side, e] = square
            cube_t[j] += cube

        rows_of(GX, edge, unroll=2)
    for slot, place, first, count, step in local_edges(rows):
        pltpu.make_async_copy(
            local_out.at[place, pl.ds(first, count)], out.at[pl.ds(first, count), slot], sem.at[place]
        ).wait()


def far_kernel(
    cols, where, blocks, diag_t, cube_t, diag_square_t, off_a, off_b, diag_a, diag_b, old,
    out, far_left, far_square, diag_out, sem,
):
    rows = blocks.shape[0]

    def one(j):
        total = cube_t[j] + dot(diag_t[j], diag_square_t[j])
        for off, diag, at in ((off_a, diag_a, 0), (off_b, diag_b, 1)):
            x_t, square, cube = remote_edge(
                cols[j, where[at]] >= 0, blocks[j, where[at]], off[j], diag_t[j], diag[j]
            )
            far_left[at, j] = x_t
            far_square[at, j] = square
            total += cube
        diag_out[j] = (3.0 * diag_square_t[j].astype(F32) - 2.0 * total).astype(BF16)

    rows_of(rows, one, unroll=2)
    copy = pltpu.make_async_copy(diag_out, out.at[:, CENTER], sem)
    copy.start()
    copy.wait()


def last_kernel(
    where, diag_t, far_left, far_square, far_a, far_b, near_left, near_square, near_a, near_b, old,
    out, far_out, near_out, sem,
):
    rows = diag_t.shape[0]
    copies = []
    for near, at, side in ((near_a, 2, 0), (near_b, 4, 1)):
        base = where[at + 1]

        def edge(e, near=near, base=base, side=side):
            near_out[side, e] = finish(diag_t[base + e], near_left[side, e], near_square[side, e], near[e])

        rows_of(GX, edge, unroll=2)
        copies.append(
            pltpu.make_async_copy(near_out.at[side], out.at[pl.ds(base, GX), where[at]], sem.at[2 + side])
        )
        copies[-1].start()
    for far, side in ((far_a, 0), (far_b, 1)):

        def edge(j, far=far, side=side):
            far_out[side, j] = finish(diag_t[j], far_left[side, j], far_square[side, j], far[j])

        rows_of(rows, edge, unroll=2)
        copies.append(pltpu.make_async_copy(far_out.at[side], out.at[:, where[side]], sem.at[side]))
        copies[-1].start()
    for copy in copies:
        copy.wait()


def on_device(density, block_cols):
    rows, _, size, _ = density.shape
    layer_dist = PLANE // rows
    row_id = lax.axis_index("row")
    layer_odd = row_id // layer_dist % 2
    strip_odd = row_id % layer_dist % 2
    slot_fa = jnp.where(layer_odd == 0, 6, 0)
    slot_na = jnp.where(strip_odd == 0, 5, 1)
    base_na = jnp.where(strip_odd == 0, rows - GX, 0)
    where = jnp.stack([slot_fa, 6 - slot_fa, slot_na, base_na, 6 - slot_na, rows - GX - base_na]).astype(jnp.int32)

    def block(*dims):
        return jax.ShapeDtypeStruct((*dims, size, size), BF16)

    def total(*dims):
        return jax.ShapeDtypeStruct((*dims, size, size), F32)

    smem = pl.BlockSpec(memory_space=pltpu.SMEM)
    vmem = pl.BlockSpec(memory_space=pltpu.VMEM)
    hbm = pl.BlockSpec(memory_space=pl.ANY)

    def call(kernel, ins, outs, out_specs, scratch, products, args, aliases=None):
        return pl.pallas_call(
            kernel,
            in_specs=ins,
            out_specs=out_specs,
            out_shape=outs,
            scratch_shapes=scratch,
            input_output_aliases=aliases or {},
            compiler_params=pltpu.CompilerParams(vmem_limit_bytes=VMEM_LIMIT),
            cost_estimate=pl.CostEstimate(
                flops=products * 2 * size**3, bytes_accessed=4 * rows * size * size * 2, transcendentals=0
            ),
        )(*args)

    def far(value, pairing):
        return matching(value, pairing, layer_dist, lax.axis_size("row"))

    def near(value, pairing):
        return matching(value, pairing, 1, layer_dist)

    def slot_of(slot):
        return lax.dynamic_index_in_dim(density, slot, 1, keepdims=False)

    def strip_of(value, base):
        return lax.dynamic_slice_in_dim(value, base, GX, 0)

    off_b = far(slot_of(6 - slot_fa), 1)
    off_a = far(slot_of(slot_fa), 0)

    diag_t = call(flip_diag_kernel, [vmem], block(rows), vmem, [], rows, [density])
    diag_b = far(diag_t, 1)
    diag_a = far(diag_t, 0)
    strips = []
    for slot, base in ((slot_na, base_na), (6 - slot_na, rows - GX - base_na)):
        strips.append(jnp.concatenate([strip_of(slot_of(slot), base), strip_of(diag_t, base)], axis=0))
    near_b = near(strips[1], 1)
    near_a = near(strips[0], 0)

    left_t, square_t, cube_t = call(
        local_kernel,
        [smem, vmem, vmem],
        [block(rows, 4), block(rows, 4), total(rows)],
        [vmem] * 3,
        [],
        12 * rows,
        [block_cols, density, diag_t],
    )
    diag_square_t = call(
        diag_square_kernel,
        [smem, smem] + [vmem] * 5,
        block(rows),
        vmem,
        [pltpu.VMEM((rows, size, size), F32)],
        7 * rows,
        [block_cols, where, density, off_a, off_b, near_a, near_b],
    )
    far_square_b = far(diag_square_t, 1)
    far_square_a = far(diag_square_t, 0)
    near_square_b = near(strip_of(diag_square_t, rows - GX - base_na), 1)
    near_square_a = near(strip_of(diag_square_t, base_na), 0)

    out, near_left, near_square, cube_t = call(
        near_kernel,
        [smem, smem] + [vmem] * 8,
        [block(rows, K), block(2, GX), block(2, GX), total(rows)],
        [hbm] + [vmem] * 3,
        [pltpu.VMEM((4, rows, size, size), BF16), pltpu.SemaphoreType.DMA((4,))],
        12 * rows,
        [block_cols, where, density, diag_t, left_t, square_t, cube_t, diag_square_t, near_a, near_b],
    )
    out, far_left, far_square = call(
        far_kernel,
        [smem, smem] + [vmem] * 8 + [hbm],
        [block(rows, K), block(2, rows), block(2, rows)],
        [hbm] + [vmem] * 2,
        [pltpu.VMEM((rows, size, size), BF16), pltpu.SemaphoreType.DMA],
        12 * rows,
        [block_cols, where, density, diag_t, cube_t, diag_square_t, off_a, off_b, diag_a, diag_b, out],
        {10: 0},
    )
    return call(
        last_kernel,
        [smem] + [vmem] * 9 + [hbm],
        block(rows, K),
        hbm,
        [
            pltpu.VMEM((2, rows, size, size), BF16),
            pltpu.VMEM((2, GX, size, size), BF16),
            pltpu.SemaphoreType.DMA((4,)),
        ],
        6 * rows,
        [
            where, diag_t, far_left, far_square, far_square_a, far_square_b,
            near_left, near_square, near_square_a, near_square_b, out,
        ],
        {10: 0},
    )


def solution(mesh):
    placed = (P(("groups", "row"), None, None, None), P(("groups", "row"), None))
    return jax.shard_map(
        on_device,
        mesh=mesh,
        in_specs=placed,
        out_specs=P(("groups", "row"), None, None, None),
        check_vma=False,
    )
```

```python
import jax
import jax.numpy as jnp
from jax import lax
from jax.experimental import pallas as pl
from jax.experimental.pallas import tpu as pltpu
from jax.sharding import PartitionSpec as P

K = 7
GX = 8
PLANE = 64
CENTER = 3
BF16 = jnp.bfloat16
F32 = jnp.float32
VMEM_LIMIT = 12 * 1024 * 1024
KERNEL_COST = 1000
STAGE_LIMIT = 58 * 1024 * 1024


def matching(value, parity, distance, period):
    count = lax.axis_size("row")
    pairs = []
    for source in range(count):
        place = source % period // distance
        step = distance if place % 2 == parity else -distance
        target = source + step
        if 0 <= target < count and target // period == source // period:
            pairs.append((source, target))
    return lax.ppermute(value, "row", pairs)


def dot(a, b):
    return jnp.dot(a, b, preferred_element_type=F32)


def masked(flag, block):
    return jnp.where(flag, block, jnp.zeros_like(block))


def in_groups(items, load, compute, store, group=16):
    for start in range(0, len(items), group):
        chunk = items[start : start + group]
        loaded = [load(item) for item in chunk]
        results = [compute(*values) for values in loaded]
        for item, result in zip(chunk, results):
            store(item, result)


def local_edges(rows):
    edges = []
    for slot, place, step in ((2, 1, -1), (4, 2, 1), (1, 0, -GX), (5, 3, GX)):
        for j in range(rows):
            k = j + step
            if 0 <= k < rows and (abs(step) == GX or k // GX == j // GX):
                edges.append((j, slot, place, k))
    return edges


def places(rows):
    row_id = lax.axis_index("row")
    layer_dist = PLANE // rows
    far_slot = jnp.where(row_id // layer_dist % 2 == 0, K - 1, 0)
    even = row_id % layer_dist % 2 == 0
    near_slot = jnp.where(even, CENTER + 2, CENTER - 2)
    near_base = jnp.where(even, rows - GX, 0)
    return (far_slot, K - 1 - far_slot), (near_slot, K - 1 - near_slot), (near_base, rows - GX - near_base)


def stage_kernel(blocks, diag_t, send_a, send_b, strip_a, strip_b, diag, sem):
    rows = blocks.shape[0]
    far_slots, near_slots, bases = places(rows)
    copies = [pltpu.make_async_copy(blocks.at[:, CENTER], diag, sem.at[0])]
    for at, send in ((1, send_b), (0, send_a)):
        copies.append(pltpu.make_async_copy(blocks.at[:, far_slots[at]], send, sem.at[1 + at]))
    for at, strip in ((1, strip_b), (0, strip_a)):
        source = blocks.at[pl.ds(bases[at], GX), near_slots[at]]
        copies.append(pltpu.make_async_copy(source, strip.at[pl.ds(0, GX)], sem.at[3 + at]))
    for copy in copies:
        copy.start()
    copies[0].wait()
    in_groups(list(range(rows)), lambda j: (diag[j],), lambda x: x.T, diag_t.__setitem__)
    for at, strip in ((1, strip_b), (0, strip_a)):
        for e in range(GX):
            strip[GX + e] = diag_t[bases[at] + e]
    for copy in copies[1:]:
        copy.wait()


def local_kernel(
    cols, blocks, diag_t, near_a, near_b,
    left_t, square_t, cube_t, near_left, near_square, total, near_right, near_other,
):
    rows = blocks.shape[0]
    edges = local_edges(rows)
    _, near_slots, bases = places(rows)
    strip = list(range(GX))

    def load(edge):
        j, slot, place, k = edge
        return cols[j, slot] >= 0, blocks[k, K - 1 - slot], diag_t[j], diag_t[k]

    def compute(flag, x, diag_own, diag_other):
        x_t = flipped(flag, x)
        return x_t, one_square(diag_own, x_t, diag_other)

    def store(edge, result):
        j, slot, place, k = edge
        left_t[place, j], square_t[place, j] = result

    in_groups(edges, load, compute, store)
    if rows != 2 * GX:
        total[...] = jnp.zeros_like(total)
        cube_t[...] = jnp.zeros_like(cube_t)
    for side, near in enumerate((near_a, near_b)):
        slot, base = near_slots[side], bases[side]

        def load_left(e):
            return cols[base + e, slot] >= 0, near[e]

        def load_right(e):
            return cols[base + e, slot] >= 0, blocks[base + e, slot]

        in_groups(strip, load_left, flipped, lambda e, value: near_left.__setitem__((side, e), value))
        in_groups(strip, load_right, flipped, lambda e, value: near_right.__setitem__((side, e), value))
        in_groups(
            strip,
            lambda e: (diag_t[base + e], near_left[side, e], near[GX + e]),
            one_square,
            lambda e, value: near_square.__setitem__((side, e), value),
        )
        in_groups(
            strip,
            lambda e: (near[GX + e], near_right[side, e], diag_t[base + e]),
            one_square,
            lambda e, value: near_other.__setitem__((side, e), value),
        )

        def load_near(e):
            j = base + e
            return near_left[side, e], near_other[side, e], near_right[side, e]

        def near_terms(x_t, square, y_t):
            return dot(x_t, square), dot(x_t, y_t)

        def store_near(e, result):
            j = base + e
            for ref, value in zip((cube_t, total), result):
                ref[j] = value if rows == 2 * GX else ref[j] + value

        in_groups(strip, load_near, near_terms, store_near)

    def load_row(j):
        own = [edge for edge in edges if edge[0] == j]
        lhs = [left_t[place, j] for _, _, place, _ in own]
        squares = [square_t[3 - place, k] for _, _, place, k in own]
        others = [left_t[3 - place, k] for _, _, place, k in own]
        return (
            jnp.concatenate(lhs, axis=1),
            jnp.concatenate(squares, axis=0),
            jnp.concatenate(lhs + [diag_t[j]], axis=1),
            jnp.concatenate(others + [diag_t[j]], axis=0),
            cube_t[j],
            total[j],
        )

    def row_terms(lhs, squares, lhs_all, others, cube, square):
        return dot(lhs, squares) + cube, dot(lhs_all, others) + square

    def store_row(j, result):
        cube_t[j], total[j] = result

    in_groups(list(range(rows)), load_row, row_terms, store_row)


def diag_square_kernel(cols, blocks, total, far_a, far_b, square_t):
    rows = blocks.shape[0]
    far_slots, _, _ = places(rows)

    def load(j):
        own = [masked(cols[j, slot] >= 0, blocks[j, slot]) for slot in far_slots]
        return jnp.concatenate(own, axis=1), jnp.concatenate([far_a[j], far_b[j]], axis=0), total[j]

    in_groups(
        list(range(rows)),
        load,
        lambda lhs, rhs, extra_t: (dot(lhs, rhs).T + extra_t).astype(BF16),
        square_t.__setitem__,
    )


def one_square(diag_own, x_t, diag_other):
    lhs = jnp.concatenate([diag_own, x_t], axis=1)
    rhs = jnp.concatenate([x_t, diag_other], axis=0)
    return dot(lhs, rhs).astype(BF16)


def finish(diag_own, x_t, square, diag_square_other):
    cube = dot(jnp.concatenate([diag_own, x_t], axis=1), jnp.concatenate([square, diag_square_other], axis=0))
    return (3.0 * square.astype(F32) - 2.0 * cube).astype(BF16)


def flipped(flag, block):
    return masked(flag, block).T


def inside_kernel(
    cols, blocks, diag_t, left_t, square_t, diag_square_t, off_a, off_b,
    out, send_a, send_b, far_left, far_right, local_out, sem,
):
    rows = blocks.shape[0]
    edges = local_edges(rows)
    far_slots, _, bases = places(rows)
    for at, send in ((1, send_b), (0, send_a)):
        for e in range(GX):
            send[e] = diag_square_t[bases[at] + e]
    copies = []
    for slot, place in ((2, 1), (4, 2), (1, 0), (5, 3)):
        own = [edge for edge in edges if edge[2] == place]
        first, last = (0, rows - 1) if abs(slot - CENTER) == 1 else (own[0][0], own[-1][0])

        def load(edge):
            j, _, _, k = edge
            return diag_t[j], left_t[place, j], square_t[place, j], diag_square_t[k]

        in_groups(own, load, finish, lambda edge, value: local_out.__setitem__((place, edge[0]), value))
        inside = [edge[0] for edge in own]
        for j in range(first, last + 1):
            if j not in inside:
                local_out[place, j] = jnp.zeros_like(diag_t[j])
        at = pl.ds(first, last + 1 - first)
        copies.append(pltpu.make_async_copy(local_out.at[place, at], out.at[at, slot], sem.at[place]))
        copies[-1].start()
    for at, off in enumerate((off_a, off_b)):
        slot = far_slots[at]
        in_groups(
            list(range(rows)),
            lambda j: (cols[j, slot] >= 0, off[j]),
            flipped,
            lambda j, value: far_left.__setitem__((at, j), value),
        )
        in_groups(
            list(range(rows)),
            lambda j: (cols[j, slot] >= 0, blocks[j, slot]),
            flipped,
            lambda j, value: far_right.__setitem__((at, j), value),
        )
    for copy in copies:
        copy.wait()


def far_kernel(
    diag_t, cube_t, diag_square_t, far_left, far_right, diag_a, diag_b, old,
    out, far_square, far_other, diag_out, sem,
):
    rows = diag_t.shape[0]
    for diag, at in ((diag_a, 0), (diag_b, 1)):
        in_groups(
            list(range(rows)),
            lambda j: (diag_t[j], far_left[at, j], diag[j]),
            one_square,
            lambda j, value: far_square.__setitem__((at, j), value),
        )
        in_groups(
            list(range(rows)),
            lambda j: (diag[j], far_right[at, j], diag_t[j]),
            one_square,
            lambda j, value: far_other.__setitem__((at, j), value),
        )

    def load(j):
        lhs = jnp.concatenate([diag_t[j], far_left[0, j], far_left[1, j]], axis=1)
        rhs = jnp.concatenate([diag_square_t[j], far_other[0, j], far_other[1, j]], axis=0)
        return lhs, rhs, cube_t[j], diag_square_t[j]

    def last(lhs, rhs, extra, square):
        return (3.0 * square.astype(F32) - 2.0 * (dot(lhs, rhs) + extra)).astype(BF16)

    in_groups(list(range(rows)), load, last, diag_out.__setitem__)
    copy = pltpu.make_async_copy(diag_out, out.at[:, CENTER], sem)
    copy.start()
    copy.wait()


def near_last_kernel(diag_t, near_left, near_square, near_a, near_b, old, out, near_out, sem):
    _, near_slots, bases = places(diag_t.shape[0])
    copies = []
    for side, near in enumerate((near_a, near_b)):
        base = bases[side]
        in_groups(
            list(range(GX)),
            lambda e: (diag_t[base + e], near_left[side, e], near_square[side, e], near[e]),
            finish,
            lambda e, value: near_out.__setitem__((side, e), value),
        )
        target = out.at[pl.ds(base, GX), near_slots[side]]
        copies.append(pltpu.make_async_copy(near_out.at[side], target, sem.at[side]))
        copies[-1].start()
    for copy in copies:
        copy.wait()


def far_last_kernel(diag_t, far_left, far_square, far_a, far_b, old, out, far_out, sem):
    rows = diag_t.shape[0]
    far_slots, _, _ = places(rows)
    copies = []
    for side, far in enumerate((far_a, far_b)):
        in_groups(
            list(range(rows)),
            lambda j: (diag_t[j], far_left[side, j], far_square[side, j], far[j]),
            finish,
            lambda j, value: far_out.__setitem__((side, j), value),
        )
        copies.append(pltpu.make_async_copy(far_out.at[side], out.at[:, far_slots[side]], sem.at[side]))
        copies[-1].start()
    for copy in copies:
        copy.wait()


def on_device(density, block_cols):
    rows, _, size, _ = density.shape
    layer_dist = PLANE // rows
    count = lax.axis_size("row")

    def block(*dims):
        return jax.ShapeDtypeStruct((*dims, size, size), BF16)

    def wide(*dims):
        return jax.ShapeDtypeStruct((*dims, size, size), F32)

    def scratch(*dims):
        return pltpu.VMEM((*dims, size, size), BF16)

    dma = pltpu.SemaphoreType.DMA
    smem = pl.BlockSpec(memory_space=pltpu.SMEM)
    vmem = pl.BlockSpec(memory_space=pltpu.VMEM)
    hbm = pl.BlockSpec(memory_space=pltpu.HBM)

    def call(kernel, in_specs, args, outs, out_specs, scratch_shapes, alias=None, vmem_limit=VMEM_LIMIT):
        return pl.pallas_call(
            kernel,
            in_specs=in_specs,
            out_specs=out_specs,
            out_shape=outs,
            scratch_shapes=scratch_shapes,
            input_output_aliases={} if alias is None else {alias: 0},
            compiler_params=pltpu.CompilerParams(vmem_limit_bytes=vmem_limit),
            cost_estimate=pl.CostEstimate(flops=0, bytes_accessed=KERNEL_COST, transcendentals=0),
        )(*args)

    def far(value, pairing):
        return matching(value, pairing, layer_dist, count)

    def near(value, pairing):
        return matching(value, pairing, 1, layer_dist)

    diag_t, send_a, send_b, strip_a, strip_b = call(
        stage_kernel,
        [hbm],
        [density],
        [block(rows), block(rows), block(rows), block(2 * GX), block(2 * GX)],
        [vmem] * 5,
        [scratch(rows), dma((5,))],
        vmem_limit=STAGE_LIMIT,
    )
    off_b = far(send_b, 1)
    off_a = far(send_a, 0)
    diag_b = far(diag_t, 1)
    diag_a = far(diag_t, 0)
    near_b = near(strip_b, 1)
    near_a = near(strip_a, 0)
    left_t, square_t, cube_t, near_left, near_square, total = call(
        local_kernel,
        [smem] + [vmem] * 4,
        [block_cols, density, diag_t, near_a, near_b],
        [block(4, rows), block(4, rows), wide(rows), block(2, GX), block(2, GX), wide(rows)],
        [vmem] * 6,
        [scratch(2, GX), scratch(2, GX)],
    )
    diag_square_t = call(
        diag_square_kernel,
        [smem] + [vmem] * 4,
        [block_cols, density, total, off_a, off_b],
        block(rows),
        vmem,
        [],
    )
    far_square_b = far(diag_square_t, 1)
    far_square_a = far(diag_square_t, 0)
    out, square_a, square_b, far_left, far_right = call(
        inside_kernel,
        [smem] + [vmem] * 7,
        [block_cols, density, diag_t, left_t, square_t, diag_square_t, off_a, off_b],
        [block(rows, K), block(GX), block(GX), block(2, rows), block(2, rows)],
        [hbm] + [vmem] * 4,
        [scratch(4, rows), dma((4,))],
    )
    near_square_b = near(square_b, 1)
    near_square_a = near(square_a, 0)
    out, far_square = call(
        far_kernel,
        [vmem] * 7 + [hbm],
        [diag_t, cube_t, diag_square_t, far_left, far_right, diag_a, diag_b, out],
        [block(rows, K), block(2, rows)],
        [hbm, vmem],
        [scratch(2, rows), scratch(rows), dma],
        alias=7,
    )
    out = call(
        near_last_kernel,
        [vmem] * 5 + [hbm],
        [diag_t, near_left, near_square, near_square_a, near_square_b, out],
        block(rows, K),
        hbm,
        [scratch(2, GX), dma((2,))],
        alias=5,
    )
    return call(
        far_last_kernel,
        [vmem] * 5 + [hbm],
        [diag_t, far_left, far_square, far_square_a, far_square_b, out],
        block(rows, K),
        hbm,
        [scratch(2, rows), dma((2,))],
        alias=5,
    )


def solution(mesh):
    placed = (P(("groups", "row"), None, None, None), P(("groups", "row"), None))
    return jax.shard_map(
        on_device,
        mesh=mesh,
        in_specs=placed,
        out_specs=P(("groups", "row"), None, None, None),
        check_vma=False,
    )
```

```python
import functools

import jax
import jax.numpy as jnp
from jax import lax
from jax.experimental import pallas as pl
from jax.experimental.pallas import tpu as pltpu
from jax.sharding import PartitionSpec as P

K = 7
GX = 8
PLANE = 64
CENTER = 3
BF16 = jnp.bfloat16
F32 = jnp.float32
VMEM_LIMIT = 12 * 1024 * 1024
STAGE_LIMIT = 50 * 1024 * 1024
KERNEL_COST = 1000


def far_pairs(pairing, layer_dist, count):
    pairs = []
    for source in range(count):
        step = layer_dist if (source // layer_dist + pairing) % 2 == 0 else -layer_dist
        if 0 <= source + step < count:
            pairs.append((source, source + step))
    return pairs


def near_pairs(pairing, layer_dist, count):
    pairs = []
    for source in range(count):
        step = 1 if (source % layer_dist + pairing) % 2 == 0 else -1
        if (source + step) // layer_dist == source // layer_dist:
            pairs.append((source, source + step))
    return pairs


def dot(a, b):
    return jnp.dot(a, b, preferred_element_type=F32)


def masked(flag, block):
    return jnp.where(flag, block, jnp.zeros_like(block))


def in_groups(items, load, compute, store, group=16):
    for start in range(0, len(items), group):
        chunk = items[start : start + group]
        loaded = [load(item) for item in chunk]
        results = [compute(*values) for values in loaded]
        for item, result in zip(chunk, results):
            store(item, result)


def local_edges(rows):
    edges = []
    for slot, place, step in ((2, 1, -1), (4, 2, 1), (1, 0, -GX), (5, 3, GX)):
        for j in range(rows):
            k = j + step
            if 0 <= k < rows and (abs(step) == GX or k // GX == j // GX):
                edges.append((j, slot, place, k))
    return edges


def places(rows):
    row_id = lax.axis_index("row")
    layer_dist = PLANE // rows
    strip = row_id % layer_dist
    far_slot = jnp.where(row_id // layer_dist % 2 == 0, K - 1, 0)
    even = strip % 2 == 0
    near_slot = jnp.where(even, CENTER + 2, CENTER - 2)
    near_base = jnp.where(even, rows - GX, 0)
    return (far_slot, K - 1 - far_slot), (near_slot, K - 1 - near_slot), (near_base, rows - GX - near_base)


def stage_kernel(blocks, send_a, send_b, strip_a, strip_b, sem):
    rows = blocks.shape[0]
    far_slots, near_slots, bases = places(rows)
    copies = []
    for at, send in ((0, send_a), (1, send_b)):
        copies.append(pltpu.make_async_copy(blocks.at[:, far_slots[at]], send, sem.at[at]))
    for at, strip in ((0, strip_a), (1, strip_b)):
        at_rows = pl.ds(bases[at], GX)
        for half, slot in enumerate((near_slots[at], CENTER)):
            part = strip.at[pl.ds(half * GX, GX)]
            copies.append(pltpu.make_async_copy(blocks.at[at_rows, slot], part, sem.at[2 + 2 * at + half]))
    for copy in copies:
        copy.start()
    for copy in copies:
        copy.wait()


def local_kernel(
    cols, blocks, near_a, near_b, strip_a, strip_b,
    diag_t, left_t, square_t, cube_t, near_left, near_square, total, near_diag, near_right, near_other,
):
    rows = diag_t.shape[0]
    in_groups(list(range(rows)), lambda j: (blocks[j, CENTER],), lambda x: x.T, diag_t.__setitem__)
    edges = local_edges(rows)
    _, near_slots, bases = places(rows)
    strip = list(range(GX))

    def load(edge):
        j, slot, place, k = edge
        return cols[slot, j] >= 0, blocks[k, K - 1 - slot], diag_t[j], diag_t[k]

    def compute(flag, x, diag_own, diag_other):
        x_t = flipped(flag, x)
        return x_t, one_square(diag_own, x_t, diag_other)

    def store(edge, result):
        j, slot, place, k = edge
        left_t[place, j], square_t[place, j] = result

    if rows != 2 * GX:
        total[...] = jnp.zeros_like(total)
        cube_t[...] = jnp.zeros_like(cube_t)
    for side, (near, own) in enumerate(((near_a, strip_a), (near_b, strip_b))):
        slot, base = near_slots[side], bases[side]

        def load_left(e):
            return cols[slot, base + e] >= 0, near[e]

        def load_right(e):
            return cols[slot, base + e] >= 0, own[e]

        in_groups(
            strip, lambda e: (near[GX + e],), lambda x: x.T, lambda e, value: near_diag.__setitem__((side, e), value)
        )
        in_groups(strip, load_left, flipped, lambda e, value: near_left.__setitem__((side, e), value))
        in_groups(strip, load_right, flipped, lambda e, value: near_right.__setitem__((side, e), value))
        in_groups(
            strip,
            lambda e: (diag_t[base + e], near_left[side, e], near_diag[side, e]),
            one_square,
            lambda e, value: near_square.__setitem__((side, e), value),
        )
        in_groups(
            strip,
            lambda e: (near_diag[side, e], near_right[side, e], diag_t[base + e]),
            one_square,
            lambda e, value: near_other.__setitem__((side, e), value),
        )

        def load_near(e):
            j = base + e
            return near_left[side, e], near_other[side, e], near_right[side, e]

        def near_terms(x_t, square, y_t):
            return dot(x_t, square), dot(x_t, y_t)

        def store_near(e, result):
            j = base + e
            for ref, value in zip((cube_t, total), result):
                ref[j] = value if rows == 2 * GX else ref[j] + value

        in_groups(strip, load_near, near_terms, store_near)

    in_groups(edges, load, compute, store)

    def load_row(j):
        own = [edge for edge in edges if edge[0] == j]
        lhs = [left_t[place, j] for _, _, place, _ in own]
        squares = [square_t[3 - place, k] for _, _, place, k in own]
        others = [left_t[3 - place, k] for _, _, place, k in own]
        return (
            jnp.concatenate(lhs, axis=1),
            jnp.concatenate(squares, axis=0),
            jnp.concatenate(lhs + [diag_t[j]], axis=1),
            jnp.concatenate(others + [diag_t[j]], axis=0),
            cube_t[j],
            total[j],
        )

    def row_terms(lhs, squares, lhs_all, others, cube, square):
        return dot(lhs, squares) + cube, dot(lhs_all, others) + square

    def store_row(j, result):
        cube_t[j], total[j] = result

    in_groups(list(range(rows)), load_row, row_terms, store_row)


def diag_square_kernel(cols, own_a, own_b, total, far_a, far_b, square_t):
    rows = total.shape[0]
    far_slots, _, _ = places(rows)

    def load(j):
        own = [masked(cols[slot, j] >= 0, own[j]) for slot, own in zip(far_slots, (own_a, own_b))]
        return jnp.concatenate(own, axis=1), jnp.concatenate([far_a[j], far_b[j]], axis=0), total[j]

    in_groups(
        list(range(rows)),
        load,
        lambda lhs, rhs, extra_t: (dot(lhs, rhs).T + extra_t).astype(BF16),
        square_t.__setitem__,
    )


def one_square(diag_own, x_t, diag_other):
    lhs = jnp.concatenate([diag_own, x_t], axis=1)
    rhs = jnp.concatenate([x_t, diag_other], axis=0)
    return dot(lhs, rhs).astype(BF16)


def finish(diag_own, x_t, square, diag_square_other):
    cube = dot(jnp.concatenate([diag_own, x_t], axis=1), jnp.concatenate([square, diag_square_other], axis=0))
    return (3.0 * square.astype(F32) - 2.0 * cube).astype(BF16)


def flipped(flag, block):
    return masked(flag, block).T


def inside_kernel(
    cols, own_a, own_b, diag_t, left_t, square_t, diag_square_t, off_a, off_b,
    out, send_a, send_b, far_left, far_right, local_out, sem,
):
    rows = diag_t.shape[0]
    edges = local_edges(rows)
    far_slots, _, bases = places(rows)
    for at, send in ((1, send_b), (0, send_a)):
        for e in range(GX):
            send[e] = diag_square_t[bases[at] + e]
    copies = []
    for slot, place in ((2, 1), (4, 2), (1, 0), (5, 3)):
        own = [edge for edge in edges if edge[2] == place]
        first, last = (0, rows - 1) if abs(slot - CENTER) == 1 else (own[0][0], own[-1][0])

        def load(edge):
            j, _, _, k = edge
            return diag_t[j], left_t[place, j], square_t[place, j], diag_square_t[k]

        in_groups(own, load, finish, lambda edge, value: local_out.__setitem__((place, edge[0]), value))
        inside = [edge[0] for edge in own]
        for j in range(first, last + 1):
            if j not in inside:
                local_out[place, j] = jnp.zeros_like(diag_t[j])
        at = pl.ds(first, last + 1 - first)
        copies.append(pltpu.make_async_copy(local_out.at[place, at], out.at[at, slot], sem.at[place]))
        copies[-1].start()
    for at, (off, own) in enumerate(((off_a, own_a), (off_b, own_b))):
        slot = far_slots[at]
        in_groups(
            list(range(rows)),
            lambda j: (cols[slot, j] >= 0, off[j]),
            flipped,
            lambda j, value: far_left.__setitem__((at, j), value),
        )
        in_groups(
            list(range(rows)),
            lambda j: (cols[slot, j] >= 0, own[j]),
            flipped,
            lambda j, value: far_right.__setitem__((at, j), value),
        )
    for copy in copies:
        copy.wait()


def far_kernel(
    diag_t, cube_t, diag_square_t, far_left, far_right, diag_a, diag_b, old,
    out, far_square, far_other, diag_out, sem,
):
    rows = diag_t.shape[0]
    for diag, at in ((diag_a, 0), (diag_b, 1)):
        in_groups(
            list(range(rows)),
            lambda j: (diag_t[j], far_left[at, j], diag[j]),
            one_square,
            lambda j, value: far_square.__setitem__((at, j), value),
        )
        in_groups(
            list(range(rows)),
            lambda j: (diag[j], far_right[at, j], diag_t[j]),
            one_square,
            lambda j, value: far_other.__setitem__((at, j), value),
        )

    def load(j):
        lhs = jnp.concatenate([diag_t[j], far_left[0, j], far_left[1, j]], axis=1)
        rhs = jnp.concatenate([diag_square_t[j], far_other[0, j], far_other[1, j]], axis=0)
        return lhs, rhs, cube_t[j], diag_square_t[j]

    def last(lhs, rhs, extra, square):
        return (3.0 * square.astype(F32) - 2.0 * (dot(lhs, rhs) + extra)).astype(BF16)

    in_groups(list(range(rows)), load, last, diag_out.__setitem__)
    copy = pltpu.make_async_copy(diag_out, out.at[:, CENTER], sem)
    copy.start()
    copy.wait()


def near_last_kernel(diag_t, near_left, near_square, near_a, near_b, old, out, near_out, sem):
    _, near_slots, bases = places(diag_t.shape[0])
    copies = []
    for side, near in enumerate((near_a, near_b)):
        base = bases[side]
        in_groups(
            list(range(GX)),
            lambda e: (diag_t[base + e], near_left[side, e], near_square[side, e], near[e]),
            finish,
            lambda e, value: near_out.__setitem__((side, e), value),
        )
        target = out.at[pl.ds(base, GX), near_slots[side]]
        copies.append(pltpu.make_async_copy(near_out.at[side], target, sem.at[side]))
        copies[-1].start()
    for copy in copies:
        copy.wait()


def far_last_kernel(side, diag_t, far_left, far_square, far, old, out, far_out, sem):
    rows = diag_t.shape[0]
    slot = places(rows)[0][side]
    copies = []
    for part in range(rows // GX):
        first = part * GX
        in_groups(
            list(range(first, first + GX)),
            lambda j: (diag_t[j], far_left[side, j], far_square[side, j], far[j]),
            finish,
            far_out.__setitem__,
        )
        at = pl.ds(first, GX)
        copies.append(pltpu.make_async_copy(far_out.at[at], out.at[at, slot], sem.at[part]))
        copies[-1].start()
    for copy in copies:
        copy.wait()


def on_device(density, block_cols):
    rows, _, size, _ = density.shape
    layer_dist = PLANE // rows
    count = lax.axis_size("row")

    def block(*dims):
        return jax.ShapeDtypeStruct((*dims, size, size), BF16)

    def wide(*dims):
        return jax.ShapeDtypeStruct((*dims, size, size), F32)

    def scratch(*dims):
        return pltpu.VMEM((*dims, size, size), BF16)

    cols = block_cols.T
    dma = pltpu.SemaphoreType.DMA
    smem = pl.BlockSpec(memory_space=pltpu.SMEM)
    vmem = pl.BlockSpec(memory_space=pltpu.VMEM)
    hbm = pl.BlockSpec(memory_space=pltpu.HBM)

    def call(kernel, in_specs, args, outs, out_specs, scratch_shapes, alias=None, vmem_limit=VMEM_LIMIT):
        return pl.pallas_call(
            kernel,
            in_specs=in_specs,
            out_specs=out_specs,
            out_shape=outs,
            scratch_shapes=scratch_shapes,
            input_output_aliases={} if alias is None else {alias: 0},
            compiler_params=pltpu.CompilerParams(vmem_limit_bytes=vmem_limit),
            cost_estimate=pl.CostEstimate(flops=0, bytes_accessed=KERNEL_COST, transcendentals=0),
        )(*args)

    def far(value, pairing):
        return lax.ppermute(value, "row", far_pairs(pairing, layer_dist, count))

    def near(value, pairing):
        return lax.ppermute(value, "row", near_pairs(pairing, layer_dist, count))

    send_a, send_b, strip_a, strip_b = call(
        stage_kernel,
        [hbm],
        [density],
        [block(rows), block(rows), block(2 * GX), block(2 * GX)],
        [vmem] * 4,
        [dma((6,))],
        vmem_limit=STAGE_LIMIT,
    )
    off_b = far(send_b, 1)
    off_a = far(send_a, 0)
    near_b = near(strip_b, 1)
    near_a = near(strip_a, 0)
    diag_t, left_t, square_t, cube_t, near_left, near_square, total = call(
        local_kernel,
        [smem] + [vmem] * 5,
        [cols, density, near_a, near_b, strip_a, strip_b],
        [block(rows), block(4, rows), block(4, rows), wide(rows), block(2, GX), block(2, GX), wide(rows)],
        [vmem] * 7,
        [scratch(2, GX)] * 3,
    )
    diag_b = far(diag_t, 1)
    diag_a = far(diag_t, 0)
    diag_square_t = call(
        diag_square_kernel,
        [smem] + [vmem] * 5,
        [cols, send_a, send_b, total, off_a, off_b],
        block(rows),
        vmem,
        [],
    )
    far_square_b = far(diag_square_t, 1)
    far_square_a = far(diag_square_t, 0)
    out, square_a, square_b, far_left, far_right = call(
        inside_kernel,
        [smem] + [vmem] * 8,
        [cols, send_a, send_b, diag_t, left_t, square_t, diag_square_t, off_a, off_b],
        [block(rows, K), block(GX), block(GX), block(2, rows), block(2, rows)],
        [hbm] + [vmem] * 4,
        [scratch(4, rows), dma((4,))],
    )
    near_square_b = near(square_b, 1)
    near_square_a = near(square_a, 0)
    out, far_square = call(
        far_kernel,
        [vmem] * 7 + [hbm],
        [diag_t, cube_t, diag_square_t, far_left, far_right, diag_a, diag_b, out],
        [block(rows, K), block(2, rows)],
        [hbm, vmem],
        [scratch(2, rows), scratch(rows), dma],
        alias=7,
    )
    out = call(
        near_last_kernel,
        [vmem] * 5 + [hbm],
        [diag_t, near_left, near_square, near_square_a, near_square_b, out],
        block(rows, K),
        hbm,
        [scratch(2, GX), dma((2,))],
        alias=5,
    )
    for side, far_diag_square in ((0, far_square_a), (1, far_square_b)):
        out = call(
            functools.partial(far_last_kernel, side),
            [vmem] * 4 + [hbm],
            [diag_t, far_left, far_square, far_diag_square, out],
            block(rows, K),
            hbm,
            [scratch(rows), dma((rows // GX,))],
            alias=4,
        )
    return out


def solution(mesh):
    placed = (P(("groups", "row"), None, None, None), P(("groups", "row"), None))
    return jax.shard_map(
        on_device,
        mesh=mesh,
        in_specs=placed,
        out_specs=P(("groups", "row"), None, None, None),
        check_vma=False,
    )
```

```python
import functools

import jax
import jax.numpy as jnp
from jax import lax
from jax.experimental import pallas as pl
from jax.experimental.pallas import tpu as pltpu
from jax.sharding import PartitionSpec as P

K = 7
GX = 8
PLANE = 64
CENTER = 3
BF16 = jnp.bfloat16
F32 = jnp.float32
VMEM_LIMIT = 12 * 1024 * 1024
STAGE_LIMIT = 50 * 1024 * 1024
KERNEL_COST = 1000


def far_pairs(pairing, layer_dist, count):
    pairs = []
    for source in range(count):
        step = layer_dist if (source // layer_dist + pairing) % 2 == 0 else -layer_dist
        if 0 <= source + step < count:
            pairs.append((source, source + step))
    return pairs


def near_pairs(pairing, layer_dist, count):
    pairs = []
    for source in range(count):
        step = 1 if (source % layer_dist + pairing) % 2 == 0 else -1
        if (source + step) // layer_dist == source // layer_dist:
            pairs.append((source, source + step))
    return pairs


def dot(a, b):
    return jnp.dot(a, b, preferred_element_type=F32)


def masked(flag, block):
    return jnp.where(flag, block, jnp.zeros_like(block))


def in_groups(items, load, compute, store, group=16):
    for start in range(0, len(items), group):
        chunk = items[start : start + group]
        loaded = [load(item) for item in chunk]
        results = [compute(*values) for values in loaded]
        for item, result in zip(chunk, results):
            store(item, result)


def local_edges(rows):
    edges = []
    for slot, place, step in ((2, 1, -1), (4, 2, 1), (1, 0, -GX), (5, 3, GX)):
        for j in range(rows):
            k = j + step
            if 0 <= k < rows and (abs(step) == GX or k // GX == j // GX):
                edges.append((j, slot, place, k))
    return edges


def places(rows):
    row_id = lax.axis_index("row")
    layer_dist = PLANE // rows
    strip = row_id % layer_dist
    far_slot = jnp.where(row_id // layer_dist % 2 == 0, K - 1, 0)
    even = strip % 2 == 0
    near_slot = jnp.where(even, CENTER + 2, CENTER - 2)
    near_base = jnp.where(even, rows - GX, 0)
    return (far_slot, K - 1 - far_slot), (near_slot, K - 1 - near_slot), (near_base, rows - GX - near_base)


def pack_kernel(blocks, send_a, send_b, sem):
    far_slots, _, _ = places(blocks.shape[0])
    copies = []
    for at, send in enumerate((send_a, send_b)):
        copies.append(pltpu.make_async_copy(blocks.at[:, far_slots[at]], send, sem.at[at]))
        copies[-1].start()
    for copy in copies:
        copy.wait()


def local_kernel(cols, blocks, diag_t, left_t, square_t, cube_t, total, strip_a, strip_b):
    rows = diag_t.shape[0]
    _, near_slots, bases = places(rows)
    in_groups(list(range(rows)), lambda j: (blocks[j, CENTER],), lambda x: x.T, diag_t.__setitem__)
    for at, strip in enumerate((strip_a, strip_b)):
        for e in range(GX):
            strip[e] = blocks[bases[at] + e, near_slots[at]]
            strip[GX + e] = diag_t[bases[at] + e]
    edges = local_edges(rows)

    def load(edge):
        j, slot, place, k = edge
        return cols[slot, j] >= 0, blocks[k, K - 1 - slot], diag_t[j], diag_t[k]

    def compute(flag, x, diag_own, diag_other):
        x_t = flipped(flag, x)
        return x_t, one_square(diag_own, x_t, diag_other)

    def store(edge, result):
        j, slot, place, k = edge
        left_t[place, j], square_t[place, j] = result

    in_groups(edges, load, compute, store)

    def load_row(j):
        own = [edge for edge in edges if edge[0] == j]
        lhs = [left_t[place, j] for _, _, place, _ in own]
        squares = [square_t[3 - place, k] for _, _, place, k in own]
        others = [left_t[3 - place, k] for _, _, place, k in own]
        return (
            jnp.concatenate(lhs, axis=1),
            jnp.concatenate(squares, axis=0),
            jnp.concatenate(lhs + [diag_t[j]], axis=1),
            jnp.concatenate(others + [diag_t[j]], axis=0),
        )

    def store_row(j, result):
        cube_t[j], total[j] = result

    in_groups(
        list(range(rows)),
        load_row,
        lambda lhs, squares, lhs_all, others: (dot(lhs, squares), dot(lhs_all, others)),
        store_row,
    )


def far_terms_kernel(cols, own_a, own_b, total, far_a, far_b, more):
    rows = total.shape[0]
    far_slots, _, _ = places(rows)

    def load(j):
        own = [masked(cols[slot, j] >= 0, own[j]) for slot, own in zip(far_slots, (own_a, own_b))]
        return jnp.concatenate(own, axis=1), jnp.concatenate([far_a[j], far_b[j]], axis=0), total[j]

    in_groups(list(range(rows)), load, lambda lhs, rhs, extra_t: dot(lhs, rhs).T + extra_t, more.__setitem__)


def near_terms_kernel(cols, strip_a, strip_b, more, near_a, near_b, square_t, near_left, near_right, total):
    rows = more.shape[0]
    _, near_slots, bases = places(rows)
    if rows != 2 * GX:
        total[...] = more[...]
    for side, (near, own) in enumerate(((near_a, strip_a), (near_b, strip_b))):
        slot, base = near_slots[side], bases[side]
        so_far = more if rows == 2 * GX else total

        def load(e):
            return cols[slot, base + e] >= 0, own[e], near[e], so_far[base + e]

        def compute(flag, y, x, extra_t):
            x_t, y_t = flipped(flag, x), flipped(flag, y)
            return x_t, y_t, dot(x_t, y_t) + extra_t

        def store(e, result):
            near_left[side, e], near_right[side, e], square = result
            if rows == 2 * GX:
                square_t[base + e] = square.astype(BF16)
            else:
                total[base + e] = square

        in_groups(list(range(GX)), load, compute, store)
    if rows != 2 * GX:
        square_t[...] = total[...].astype(BF16)


def one_square(diag_own, x_t, diag_other):
    lhs = jnp.concatenate([diag_own, x_t], axis=1)
    rhs = jnp.concatenate([x_t, diag_other], axis=0)
    return dot(lhs, rhs).astype(BF16)


def finish(diag_own, x_t, square, diag_square_other):
    cube = dot(jnp.concatenate([diag_own, x_t], axis=1), jnp.concatenate([square, diag_square_other], axis=0))
    return (3.0 * square.astype(F32) - 2.0 * cube).astype(BF16)


def flipped(flag, block):
    return masked(flag, block).T


def inside_kernel(
    cols, own_a, own_b, diag_t, left_t, square_t, cube_in, diag_square_t, off_a, off_b,
    near_a, near_b, near_left, near_right,
    out, send_a, send_b, far_left, far_right, near_square, cube_t, local_out, near_other, sem,
):
    rows = diag_t.shape[0]
    edges = local_edges(rows)
    far_slots, _, bases = places(rows)
    for at, send in ((1, send_b), (0, send_a)):
        for e in range(GX):
            send[e] = diag_square_t[bases[at] + e]
    copies = []
    for slot, place in ((2, 1), (4, 2), (1, 0), (5, 3)):
        own = [edge for edge in edges if edge[2] == place]
        first, last = (0, rows - 1) if abs(slot - CENTER) == 1 else (own[0][0], own[-1][0])

        def load(edge):
            j, _, _, k = edge
            return diag_t[j], left_t[place, j], square_t[place, j], diag_square_t[k]

        in_groups(own, load, finish, lambda edge, value: local_out.__setitem__((place, edge[0]), value))
        inside = [edge[0] for edge in own]
        for j in range(first, last + 1):
            if j not in inside:
                local_out[place, j] = jnp.zeros_like(diag_t[j])
        at = pl.ds(first, last + 1 - first)
        copies.append(pltpu.make_async_copy(local_out.at[place, at], out.at[at, slot], sem.at[place]))
        copies[-1].start()
    if rows != 2 * GX:
        cube_t[...] = cube_in[...]
    strip = list(range(GX))
    for side, near in enumerate((near_a, near_b)):
        base = bases[side]
        so_far = cube_in if rows == 2 * GX else cube_t
        in_groups(
            strip,
            lambda e: (diag_t[base + e], near_left[side, e], near[GX + e]),
            one_square,
            lambda e, value: near_square.__setitem__((side, e), value),
        )
        in_groups(
            strip,
            lambda e: (near[GX + e], near_right[side, e], diag_t[base + e]),
            one_square,
            lambda e, value: near_other.__setitem__((side, e), value),
        )
        in_groups(
            strip,
            lambda e: (near_left[side, e], near_other[side, e], so_far[base + e]),
            lambda x_t, square, extra: dot(x_t, square) + extra,
            lambda e, value: cube_t.__setitem__(base + e, value),
        )
    for at, (off, own) in enumerate(((off_a, own_a), (off_b, own_b))):
        slot = far_slots[at]
        in_groups(
            list(range(rows)),
            lambda j: (cols[slot, j] >= 0, off[j]),
            flipped,
            lambda j, value: far_left.__setitem__((at, j), value),
        )
        in_groups(
            list(range(rows)),
            lambda j: (cols[slot, j] >= 0, own[j]),
            flipped,
            lambda j, value: far_right.__setitem__((at, j), value),
        )
    for copy in copies:
        copy.wait()


def far_kernel(
    diag_t, cube_t, diag_square_t, far_left, far_right, diag_a, diag_b, old,
    out, far_square, far_other, diag_out, sem,
):
    rows = diag_t.shape[0]
    for diag, at in ((diag_a, 0), (diag_b, 1)):
        in_groups(
            list(range(rows)),
            lambda j: (diag_t[j], far_left[at, j], diag[j]),
            one_square,
            lambda j, value: far_square.__setitem__((at, j), value),
        )
        in_groups(
            list(range(rows)),
            lambda j: (diag[j], far_right[at, j], diag_t[j]),
            one_square,
            lambda j, value: far_other.__setitem__((at, j), value),
        )

    def load(j):
        lhs = jnp.concatenate([diag_t[j], far_left[0, j], far_left[1, j]], axis=1)
        rhs = jnp.concatenate([diag_square_t[j], far_other[0, j], far_other[1, j]], axis=0)
        return lhs, rhs, cube_t[j], diag_square_t[j]

    def last(lhs, rhs, extra, square):
        return (3.0 * square.astype(F32) - 2.0 * (dot(lhs, rhs) + extra)).astype(BF16)

    in_groups(list(range(rows)), load, last, diag_out.__setitem__)
    copy = pltpu.make_async_copy(diag_out, out.at[:, CENTER], sem)
    copy.start()
    copy.wait()


def near_last_kernel(diag_t, near_left, near_square, near_a, near_b, old, out, near_out, sem):
    _, near_slots, bases = places(diag_t.shape[0])
    copies = []
    for side, near in enumerate((near_a, near_b)):
        base = bases[side]
        in_groups(
            list(range(GX)),
            lambda e: (diag_t[base + e], near_left[side, e], near_square[side, e], near[e]),
            finish,
            lambda e, value: near_out.__setitem__((side, e), value),
        )
        target = out.at[pl.ds(base, GX), near_slots[side]]
        copies.append(pltpu.make_async_copy(near_out.at[side], target, sem.at[side]))
        copies[-1].start()
    for copy in copies:
        copy.wait()


def far_last_kernel(side, diag_t, far_left, far_square, far, old, out, far_out, sem):
    rows = diag_t.shape[0]
    slot = places(rows)[0][side]
    copies = []
    for part in range(rows // GX):
        first = part * GX
        in_groups(
            list(range(first, first + GX)),
            lambda j: (diag_t[j], far_left[side, j], far_square[side, j], far[j]),
            finish,
            far_out.__setitem__,
        )
        at = pl.ds(first, GX)
        copies.append(pltpu.make_async_copy(far_out.at[at], out.at[at, slot], sem.at[part]))
        copies[-1].start()
    for copy in copies:
        copy.wait()


def on_device(density, block_cols):
    rows, _, size, _ = density.shape
    layer_dist = PLANE // rows
    count = lax.axis_size("row")

    def block(*dims):
        return jax.ShapeDtypeStruct((*dims, size, size), BF16)

    def wide(*dims):
        return jax.ShapeDtypeStruct((*dims, size, size), F32)

    def scratch(*dims):
        return pltpu.VMEM((*dims, size, size), BF16)

    cols = block_cols.T
    dma = pltpu.SemaphoreType.DMA
    smem = pl.BlockSpec(memory_space=pltpu.SMEM)
    vmem = pl.BlockSpec(memory_space=pltpu.VMEM)
    hbm = pl.BlockSpec(memory_space=pltpu.HBM)

    def call(kernel, in_specs, args, outs, out_specs, scratch_shapes, alias=None, vmem_limit=VMEM_LIMIT):
        return pl.pallas_call(
            kernel,
            in_specs=in_specs,
            out_specs=out_specs,
            out_shape=outs,
            scratch_shapes=scratch_shapes,
            input_output_aliases={} if alias is None else {alias: 0},
            compiler_params=pltpu.CompilerParams(vmem_limit_bytes=vmem_limit),
            cost_estimate=pl.CostEstimate(flops=0, bytes_accessed=KERNEL_COST, transcendentals=0),
        )(*args)

    def far(value, pairing):
        return lax.ppermute(value, "row", far_pairs(pairing, layer_dist, count))

    def near(value, pairing):
        return lax.ppermute(value, "row", near_pairs(pairing, layer_dist, count))

    send_a, send_b = call(
        pack_kernel,
        [hbm],
        [density],
        [block(rows), block(rows)],
        [vmem] * 2,
        [dma((2,))],
        vmem_limit=STAGE_LIMIT,
    )
    off_b = far(send_b, 1)
    off_a = far(send_a, 0)
    diag_t, left_t, square_t, cube_t, total, strip_a, strip_b = call(
        local_kernel,
        [smem, vmem],
        [cols, density],
        [
            block(rows), block(4, rows), block(4, rows), wide(rows), wide(rows), block(2 * GX), block(2 * GX),
        ],
        [vmem] * 7,
        [],
    )
    diag_b = far(diag_t, 1)
    diag_a = far(diag_t, 0)
    near_b = near(strip_b, 1)
    near_a = near(strip_a, 0)
    total = call(
        far_terms_kernel,
        [smem] + [vmem] * 5,
        [cols, send_a, send_b, total, off_a, off_b],
        wide(rows),
        vmem,
        [],
    )
    diag_square_t, near_left, near_right = call(
        near_terms_kernel,
        [smem] + [vmem] * 5,
        [cols, strip_a, strip_b, total, near_a, near_b],
        [block(rows), block(2, GX), block(2, GX)],
        [vmem] * 3,
        [pltpu.VMEM((rows, size, size), F32)],
    )
    far_square_b = far(diag_square_t, 1)
    far_square_a = far(diag_square_t, 0)
    out, square_a, square_b, far_left, far_right, near_square, cube_t = call(
        inside_kernel,
        [smem] + [vmem] * 13,
        [
            cols, send_a, send_b, diag_t, left_t, square_t, cube_t, diag_square_t, off_a, off_b,
            near_a, near_b, near_left, near_right,
        ],
        [
            block(rows, K), block(GX), block(GX), block(2, rows), block(2, rows), block(2, GX), wide(rows),
        ],
        [hbm] + [vmem] * 6,
        [scratch(4, rows), scratch(2, GX), dma((4,))],
    )
    near_square_b = near(square_b, 1)
    near_square_a = near(square_a, 0)
    out, far_square = call(
        far_kernel,
        [vmem] * 7 + [hbm],
        [diag_t, cube_t, diag_square_t, far_left, far_right, diag_a, diag_b, out],
        [block(rows, K), block(2, rows)],
        [hbm, vmem],
        [scratch(2, rows), scratch(rows), dma],
        alias=7,
    )
    out = call(
        near_last_kernel,
        [vmem] * 5 + [hbm],
        [diag_t, near_left, near_square, near_square_a, near_square_b, out],
        block(rows, K),
        hbm,
        [scratch(2, GX), dma((2,))],
        alias=5,
    )
    for side, far_diag_square in ((0, far_square_a), (1, far_square_b)):
        out = call(
            functools.partial(far_last_kernel, side),
            [vmem] * 4 + [hbm],
            [diag_t, far_left, far_square, far_diag_square, out],
            block(rows, K),
            hbm,
            [scratch(rows), dma((rows // GX,))],
            alias=4,
        )
    return out


def solution(mesh):
    placed = (P(("groups", "row"), None, None, None), P(("groups", "row"), None))
    return jax.shard_map(
        on_device,
        mesh=mesh,
        in_specs=placed,
        out_specs=P(("groups", "row"), None, None, None),
        check_vma=False,
    )
```

```python
import functools

import jax
import jax.numpy as jnp
from jax import lax
from jax.experimental import pallas as pl
from jax.experimental.pallas import tpu as pltpu
from jax.sharding import PartitionSpec as P

K = 7
GX = 8
PLANE = 64
CENTER = 3
BF16 = jnp.bfloat16
F32 = jnp.float32
VMEM_LIMIT = 12 * 1024 * 1024
STAGE_LIMIT = 50 * 1024 * 1024
KERNEL_COST = 1000
SPARE = 16


def far_pairs(pairing, layer_dist, count):
    pairs = []
    for source in range(count):
        step = layer_dist if (source // layer_dist + pairing) % 2 == 0 else -layer_dist
        if 0 <= source + step < count:
            pairs.append((source, source + step))
    return pairs


def near_pairs(pairing, layer_dist, count):
    pairs = []
    for source in range(count):
        step = 1 if (source % layer_dist + pairing) % 2 == 0 else -1
        if (source + step) // layer_dist == source // layer_dist:
            pairs.append((source, source + step))
    return pairs


def dot(a, b):
    return jnp.dot(a, b, preferred_element_type=F32)


def masked(flag, block):
    return jnp.where(flag, block, jnp.zeros_like(block))


def in_groups(items, load, compute, store, group=16):
    for start in range(0, len(items), group):
        chunk = items[start : start + group]
        loaded = [load(item) for item in chunk]
        results = [compute(*values) for values in loaded]
        for item, result in zip(chunk, results):
            store(item, result)


def local_edges(rows):
    edges = []
    for slot, place, step in ((2, 1, -1), (4, 2, 1), (1, 0, -GX), (5, 3, GX)):
        for j in range(rows):
            k = j + step
            if 0 <= k < rows and (abs(step) == GX or k // GX == j // GX):
                edges.append((j, slot, place, k))
    return edges


def places(rows):
    row_id = lax.axis_index("row")
    layer_dist = PLANE // rows
    strip = row_id % layer_dist
    far_slot = jnp.where(row_id // layer_dist % 2 == 0, K - 1, 0)
    even = strip % 2 == 0
    near_slot = jnp.where(even, CENTER + 2, CENTER - 2)
    near_base = jnp.where(even, rows - GX, 0)
    return (far_slot, K - 1 - far_slot), (near_slot, K - 1 - near_slot), (near_base, rows - GX - near_base)


def packed(ref, j):
    size = ref.shape[1]
    return ref.at[pl.ds(j * size, size)]


def pack_kernel(blocks, send_a, send_b, sem):
    rows = blocks.shape[0]
    far_slots, _, _ = places(rows)
    copies = []
    for at, send in enumerate((send_a, send_b)):
        size = send.shape[1]
        target = send.at[pl.ds(0, rows * size)].reshape(rows, size, size)
        copies.append(pltpu.make_async_copy(blocks.at[:, far_slots[at]], target, sem.at[at]))
        copies[-1].start()
        spare = pl.ds(rows * send.shape[1], SPARE)
        send[spare] = jnp.zeros((SPARE, send.shape[1]), BF16)
    for copy in copies:
        copy.wait()


def local_kernel(cols, blocks, diag_t, diag_send, left_t, square_t, cube_t, total, strip_a, strip_b):
    rows = diag_t.shape[0]
    _, near_slots, bases = places(rows)
    in_groups(list(range(rows)), lambda j: (blocks[j, CENTER],), lambda x: x.T, diag_t.__setitem__)
    size = diag_send.shape[1]
    for j in range(rows):
        diag_send[pl.ds(j * size, size)] = diag_t[j]
    diag_send[pl.ds(rows * size, SPARE)] = jnp.zeros((SPARE, size), BF16)
    for at, strip in enumerate((strip_a, strip_b)):
        for e in range(GX):
            strip[e] = blocks[bases[at] + e, near_slots[at]]
            strip[GX + e] = diag_t[bases[at] + e]
    edges = local_edges(rows)

    def load(edge):
        j, slot, place, k = edge
        return cols[slot, j] >= 0, blocks[k, K - 1 - slot], diag_t[j], diag_t[k]

    def compute(flag, x, diag_own, diag_other):
        x_t = flipped(flag, x)
        return x_t, one_square(diag_own, x_t, diag_other)

    def store(edge, result):
        j, slot, place, k = edge
        left_t[place, j], square_t[place, j] = result

    in_groups(edges, load, compute, store)

    def load_row(j):
        own = [edge for edge in edges if edge[0] == j]
        lhs = [left_t[place, j] for _, _, place, _ in own]
        squares = [square_t[3 - place, k] for _, _, place, k in own]
        others = [left_t[3 - place, k] for _, _, place, k in own]
        return (
            jnp.concatenate(lhs, axis=1),
            jnp.concatenate(squares, axis=0),
            jnp.concatenate(lhs + [diag_t[j]], axis=1),
            jnp.concatenate(others + [diag_t[j]], axis=0),
        )

    def store_row(j, result):
        cube_t[j], total[j] = result

    in_groups(
        list(range(rows)),
        load_row,
        lambda lhs, squares, lhs_all, others: (dot(lhs, squares), dot(lhs_all, others)),
        store_row,
    )


def diag_square_kernel(
    cols, strip_a, strip_b, own_a, own_b, local, near_a, near_b, far_a, far_b,
    square_t, near_left, near_right, square_a, square_b, total,
):
    rows = local.shape[0]
    far_slots, near_slots, bases = places(rows)
    if rows != 2 * GX:
        total[...] = local[...]
    for side, (near, own) in enumerate(((near_a, strip_a), (near_b, strip_b))):
        slot, base = near_slots[side], bases[side]
        so_far = local if rows == 2 * GX else total

        def load(e):
            return cols[slot, base + e] >= 0, own[e], near[e], so_far[base + e]

        def compute(flag, y, x, extra_t):
            x_t, y_t = flipped(flag, x), flipped(flag, y)
            return x_t, y_t, dot(x_t, y_t) + extra_t

        def store(e, result):
            near_left[side, e], near_right[side, e], total[base + e] = result

        in_groups(list(range(GX)), load, compute, store)

    def load_far(j):
        own = [masked(cols[slot, j] >= 0, packed(own, j)[...]) for slot, own in zip(far_slots, (own_a, own_b))]
        return jnp.concatenate(own, axis=1), jnp.concatenate([packed(far_a, j)[...], packed(far_b, j)[...]], axis=0), total[j]

    in_groups(
        list(range(rows)),
        load_far,
        lambda lhs, rhs, extra_t: (dot(lhs, rhs).T + extra_t).astype(BF16),
        square_t.__setitem__,
    )
    for at, send in enumerate((square_a, square_b)):
        for e in range(GX):
            send[e] = square_t[bases[at] + e]


def one_square(diag_own, x_t, diag_other):
    lhs = jnp.concatenate([diag_own, x_t], axis=1)
    rhs = jnp.concatenate([x_t, diag_other], axis=0)
    return dot(lhs, rhs).astype(BF16)


def finish(diag_own, x_t, square, diag_square_other):
    cube = dot(jnp.concatenate([diag_own, x_t], axis=1), jnp.concatenate([square, diag_square_other], axis=0))
    return (3.0 * square.astype(F32) - 2.0 * cube).astype(BF16)


def flipped(flag, block):
    return masked(flag, block).T


def inside_kernel(
    cols, own_a, own_b, diag_t, left_t, square_t, cube_in, diag_square_t, off_a, off_b,
    near_a, near_b, near_left, near_right,
    out, far_left, far_right, near_square, cube_t, local_out, near_other, sem,
):
    rows = diag_t.shape[0]
    edges = local_edges(rows)
    far_slots, _, bases = places(rows)
    copies = []
    for slot, place in ((2, 1), (4, 2), (1, 0), (5, 3)):
        own = [edge for edge in edges if edge[2] == place]
        first, last = (0, rows - 1) if abs(slot - CENTER) == 1 else (own[0][0], own[-1][0])

        def load(edge):
            j, _, _, k = edge
            return diag_t[j], left_t[place, j], square_t[place, j], diag_square_t[k]

        in_groups(own, load, finish, lambda edge, value: local_out.__setitem__((place, edge[0]), value))
        inside = [edge[0] for edge in own]
        for j in range(first, last + 1):
            if j not in inside:
                local_out[place, j] = jnp.zeros_like(diag_t[j])
        at = pl.ds(first, last + 1 - first)
        copies.append(pltpu.make_async_copy(local_out.at[place, at], out.at[at, slot], sem.at[place]))
        copies[-1].start()
    if rows != 2 * GX:
        cube_t[...] = cube_in[...]
    strip = list(range(GX))
    for side, near in enumerate((near_a, near_b)):
        base = bases[side]
        so_far = cube_in if rows == 2 * GX else cube_t
        in_groups(
            strip,
            lambda e: (diag_t[base + e], near_left[side, e], near[GX + e]),
            one_square,
            lambda e, value: near_square.__setitem__((side, e), value),
        )
        in_groups(
            strip,
            lambda e: (near[GX + e], near_right[side, e], diag_t[base + e]),
            one_square,
            lambda e, value: near_other.__setitem__((side, e), value),
        )
        in_groups(
            strip,
            lambda e: (near_left[side, e], near_other[side, e], so_far[base + e]),
            lambda x_t, square, extra: dot(x_t, square) + extra,
            lambda e, value: cube_t.__setitem__(base + e, value),
        )
    for at, (off, own) in enumerate(((off_a, own_a), (off_b, own_b))):
        slot = far_slots[at]
        in_groups(
            list(range(rows)),
            lambda j: (cols[slot, j] >= 0, packed(off, j)[...]),
            flipped,
            lambda j, value: far_left.__setitem__((at, j), value),
        )
        in_groups(
            list(range(rows)),
            lambda j: (cols[slot, j] >= 0, packed(own, j)[...]),
            flipped,
            lambda j, value: far_right.__setitem__((at, j), value),
        )
    for copy in copies:
        copy.wait()


def far_kernel(
    diag_t, cube_t, diag_square_t, far_left, far_right, diag_a, diag_b, old,
    out, far_square, far_other, diag_out, sem,
):
    rows = diag_t.shape[0]
    for at, diag in enumerate((diag_a, diag_b)):
        in_groups(
            list(range(rows)),
            lambda j: (diag_t[j], far_left[at, j], packed(diag, j)[...]),
            one_square,
            lambda j, value: far_square.__setitem__((at, j), value),
        )
        in_groups(
            list(range(rows)),
            lambda j: (packed(diag, j)[...], far_right[at, j], diag_t[j]),
            one_square,
            lambda j, value: far_other.__setitem__((at, j), value),
        )

    def load(j):
        lhs = jnp.concatenate([diag_t[j], far_left[0, j], far_left[1, j]], axis=1)
        rhs = jnp.concatenate([diag_square_t[j], far_other[0, j], far_other[1, j]], axis=0)
        return lhs, rhs, cube_t[j], diag_square_t[j]

    def last(lhs, rhs, extra, square):
        return (3.0 * square.astype(F32) - 2.0 * (dot(lhs, rhs) + extra)).astype(BF16)

    in_groups(list(range(rows)), load, last, diag_out.__setitem__)
    copy = pltpu.make_async_copy(diag_out, out.at[:, CENTER], sem)
    copy.start()
    copy.wait()


def near_last_kernel(diag_t, near_left, near_square, near_a, near_b, old, out, near_out, sem):
    _, near_slots, bases = places(diag_t.shape[0])
    copies = []
    for side, near in enumerate((near_a, near_b)):
        base = bases[side]
        in_groups(
            list(range(GX)),
            lambda e: (diag_t[base + e], near_left[side, e], near_square[side, e], near[e]),
            finish,
            lambda e, value: near_out.__setitem__((side, e), value),
        )
        target = out.at[pl.ds(base, GX), near_slots[side]]
        copies.append(pltpu.make_async_copy(near_out.at[side], target, sem.at[side]))
        copies[-1].start()
    for copy in copies:
        copy.wait()


def far_last_kernel(side, diag_t, far_left, far_square, far, old, out, far_out, sem):
    rows = diag_t.shape[0]
    slot = places(rows)[0][side]
    copies = []
    for part in range(rows // GX):
        first = part * GX
        in_groups(
            list(range(first, first + GX)),
            lambda j: (diag_t[j], far_left[side, j], far_square[side, j], far[j]),
            finish,
            far_out.__setitem__,
        )
        at = pl.ds(first, GX)
        copies.append(pltpu.make_async_copy(far_out.at[at], out.at[at, slot], sem.at[part]))
        copies[-1].start()
    for copy in copies:
        copy.wait()


def on_device(density, block_cols):
    rows, _, size, _ = density.shape
    layer_dist = PLANE // rows
    count = lax.axis_size("row")

    def block(*dims):
        return jax.ShapeDtypeStruct((*dims, size, size), BF16)

    def wide(*dims):
        return jax.ShapeDtypeStruct((*dims, size, size), F32)

    def scratch(*dims):
        return pltpu.VMEM((*dims, size, size), BF16)

    cols = block_cols.T
    dma = pltpu.SemaphoreType.DMA
    smem = pl.BlockSpec(memory_space=pltpu.SMEM)
    vmem = pl.BlockSpec(memory_space=pltpu.VMEM)
    hbm = pl.BlockSpec(memory_space=pltpu.HBM)

    def call(kernel, in_specs, args, outs, out_specs, scratch_shapes, alias=None, vmem_limit=VMEM_LIMIT):
        return pl.pallas_call(
            kernel,
            in_specs=in_specs,
            out_specs=out_specs,
            out_shape=outs,
            scratch_shapes=scratch_shapes,
            input_output_aliases={} if alias is None else {alias: 0},
            compiler_params=pltpu.CompilerParams(vmem_limit_bytes=vmem_limit),
            cost_estimate=pl.CostEstimate(flops=0, bytes_accessed=KERNEL_COST, transcendentals=0),
        )(*args)

    def far(value, pairing):
        return lax.ppermute(value, "row", far_pairs(pairing, layer_dist, count))

    def near(value, pairing):
        return lax.ppermute(value, "row", near_pairs(pairing, layer_dist, count))

    rows_and_spare = jax.ShapeDtypeStruct((rows * size + SPARE, size), BF16)
    send_a, send_b = call(
        pack_kernel,
        [hbm],
        [density],
        [rows_and_spare] * 2,
        [vmem] * 2,
        [dma((2,))],
        vmem_limit=STAGE_LIMIT,
    )
    off_b = far(send_b, 1)
    off_a = far(send_a, 0)
    diag_t, diag_send, left_t, square_t, cube_t, total, strip_a, strip_b = call(
        local_kernel,
        [smem, vmem],
        [cols, density],
        [
            block(rows), rows_and_spare, block(4, rows), block(4, rows), wide(rows), wide(rows),
            block(2 * GX), block(2 * GX),
        ],
        [vmem] * 8,
        [],
    )
    diag_b = far(diag_send, 1)
    diag_a = far(diag_send, 0)
    near_b = near(strip_b, 1)
    near_a = near(strip_a, 0)
    diag_square_t, near_left, near_right, square_a, square_b = call(
        diag_square_kernel,
        [smem] + [vmem] * 9,
        [cols, strip_a, strip_b, send_a, send_b, total, near_a, near_b, off_a, off_b],
        [block(rows), block(2, GX), block(2, GX), block(GX), block(GX)],
        [vmem] * 5,
        [pltpu.VMEM((rows, size, size), F32)],
    )
    far_square_b = far(diag_square_t, 1)
    far_square_a = far(diag_square_t, 0)
    near_square_b = near(square_b, 1)
    near_square_a = near(square_a, 0)
    out, far_left, far_right, near_square, cube_t = call(
        inside_kernel,
        [smem] + [vmem] * 13,
        [
            cols, send_a, send_b, diag_t, left_t, square_t, cube_t, diag_square_t, off_a, off_b,
            near_a, near_b, near_left, near_right,
        ],
        [
            block(rows, K), block(2, rows), block(2, rows), block(2, GX), wide(rows),
        ],
        [hbm] + [vmem] * 4,
        [scratch(4, rows), scratch(2, GX), dma((4,))],
    )
    out = call(
        near_last_kernel,
        [vmem] * 5 + [hbm],
        [diag_t, near_left, near_square, near_square_a, near_square_b, out],
        block(rows, K),
        hbm,
        [scratch(2, GX), dma((2,))],
        alias=5,
    )
    out, far_square = call(
        far_kernel,
        [vmem] * 7 + [hbm],
        [diag_t, cube_t, diag_square_t, far_left, far_right, diag_a, diag_b, out],
        [block(rows, K), block(2, rows)],
        [hbm, vmem],
        [scratch(2, rows), scratch(rows), dma],
        alias=7,
    )
    for side, far_diag_square in ((0, far_square_a), (1, far_square_b)):
        out = call(
            functools.partial(far_last_kernel, side),
            [vmem] * 4 + [hbm],
            [diag_t, far_left, far_square, far_diag_square, out],
            block(rows, K),
            hbm,
            [scratch(rows), dma((rows // GX,))],
            alias=4,
        )
    return out


def solution(mesh):
    placed = (P(("groups", "row"), None, None, None), P(("groups", "row"), None))
    return jax.shard_map(
        on_device,
        mesh=mesh,
        in_specs=placed,
        out_specs=P(("groups", "row"), None, None, None),
        check_vma=False,
    )
```

```python
import functools

import jax
import jax.numpy as jnp
from jax import lax
from jax.experimental import pallas as pl
from jax.experimental.pallas import tpu as pltpu
from jax.sharding import PartitionSpec as P

K = 7
GX = 8
PLANE = 64
CENTER = 3
BF16 = jnp.bfloat16
F32 = jnp.float32
VMEM_LIMIT = 12 * 1024 * 1024
STAGE_LIMIT = 50 * 1024 * 1024
KERNEL_COST = 1000
SPARE = 16


def far_pairs(pairing, layer_dist, count):
    pairs = []
    for source in range(count):
        step = layer_dist if (source // layer_dist + pairing) % 2 == 0 else -layer_dist
        if 0 <= source + step < count:
            pairs.append((source, source + step))
    return pairs


def near_pairs(pairing, layer_dist, count):
    pairs = []
    for source in range(count):
        step = 1 if (source % layer_dist + pairing) % 2 == 0 else -1
        if (source + step) // layer_dist == source // layer_dist:
            pairs.append((source, source + step))
    return pairs


def dot(a, b):
    return jnp.dot(a, b, preferred_element_type=F32)


def masked(flag, block):
    return jnp.where(flag, block, jnp.zeros_like(block))


def in_groups(items, load, compute, store, group=16):
    for start in range(0, len(items), group):
        chunk = items[start : start + group]
        loaded = [load(item) for item in chunk]
        results = [compute(*values) for values in loaded]
        for item, result in zip(chunk, results):
            store(item, result)


def local_edges(rows):
    edges = []
    for slot, place, step in ((2, 1, -1), (4, 2, 1), (1, 0, -GX), (5, 3, GX)):
        for j in range(rows):
            k = j + step
            if 0 <= k < rows and (abs(step) == GX or k // GX == j // GX):
                edges.append((j, slot, place, k))
    return edges


def places(rows):
    row_id = lax.axis_index("row")
    layer_dist = PLANE // rows
    strip = row_id % layer_dist
    far_slot = jnp.where(row_id // layer_dist % 2 == 0, K - 1, 0)
    even = strip % 2 == 0
    near_slot = jnp.where(even, CENTER + 2, CENTER - 2)
    near_base = jnp.where(even, rows - GX, 0)
    return (far_slot, K - 1 - far_slot), (near_slot, K - 1 - near_slot), (near_base, rows - GX - near_base)


def packed(ref, j):
    size = ref.shape[1]
    return ref.at[pl.ds(j * size, size)]


def pack_kernel(blocks, send_a, send_b, sem):
    rows = blocks.shape[0]
    far_slots, _, _ = places(rows)
    copies = []
    for at, send in enumerate((send_a, send_b)):
        size = send.shape[1]
        target = send.at[pl.ds(0, rows * size)].reshape(rows, size, size)
        copies.append(pltpu.make_async_copy(blocks.at[:, far_slots[at]], target, sem.at[at]))
        copies[-1].start()
        spare = pl.ds(rows * send.shape[1], SPARE)
        send[spare] = jnp.zeros((SPARE, send.shape[1]), BF16)
    for copy in copies:
        copy.wait()


def local_kernel(cols, blocks, diag_t, diag_send, left_t, square_t, cube_t, total, strip_a, strip_b):
    rows = diag_t.shape[0]
    _, near_slots, bases = places(rows)
    in_groups(list(range(rows)), lambda j: (blocks[j, CENTER],), lambda x: x.T, diag_t.__setitem__)
    size = diag_send.shape[1]
    for j in range(rows):
        diag_send[pl.ds(j * size, size)] = diag_t[j]
    diag_send[pl.ds(rows * size, SPARE)] = jnp.zeros((SPARE, size), BF16)
    for at, strip in enumerate((strip_a, strip_b)):
        for e in range(GX):
            strip[e] = blocks[bases[at] + e, near_slots[at]]
            strip[GX + e] = diag_t[bases[at] + e]
    edges = local_edges(rows)

    def load(edge):
        j, slot, place, k = edge
        return cols[slot, j] >= 0, blocks[k, K - 1 - slot], diag_t[j], diag_t[k]

    def compute(flag, x, diag_own, diag_other):
        x_t = flipped(flag, x)
        return x_t, one_square(diag_own, x_t, diag_other)

    def store(edge, result):
        j, slot, place, k = edge
        left_t[place, j], square_t[place, j] = result

    in_groups(edges, load, compute, store)

    def load_row(j):
        own = [edge for edge in edges if edge[0] == j]
        lhs = [left_t[place, j] for _, _, place, _ in own]
        squares = [square_t[3 - place, k] for _, _, place, k in own]
        others = [left_t[3 - place, k] for _, _, place, k in own]
        return (
            jnp.concatenate(lhs, axis=1),
            jnp.concatenate(squares, axis=0),
            jnp.concatenate(lhs + [diag_t[j]], axis=1),
            jnp.concatenate(others + [diag_t[j]], axis=0),
        )

    def store_row(j, result):
        cube_t[j], total[j] = result

    in_groups(
        list(range(rows)),
        load_row,
        lambda lhs, squares, lhs_all, others: (dot(lhs, squares), dot(lhs_all, others)),
        store_row,
    )


def diag_square_kernel(
    cols, strip_a, strip_b, own_a, own_b, local, near_a, near_b, far_a, far_b,
    square_t, near_left, near_right, square_a, square_b, total,
):
    rows = local.shape[0]
    far_slots, near_slots, bases = places(rows)
    if rows != 2 * GX:
        total[...] = local[...]
    for side, (near, own) in enumerate(((near_a, strip_a), (near_b, strip_b))):
        slot, base = near_slots[side], bases[side]
        so_far = local if rows == 2 * GX else total

        def load(e):
            return cols[slot, base + e] >= 0, own[e], near[e], so_far[base + e]

        def compute(flag, y, x, extra_t):
            x_t, y_t = flipped(flag, x), flipped(flag, y)
            return x_t, y_t, dot(x_t, y_t) + extra_t

        def store(e, result):
            near_left[side, e], near_right[side, e], total[base + e] = result

        in_groups(list(range(GX)), load, compute, store)

    def load_far(j):
        own = [masked(cols[slot, j] >= 0, packed(own, j)[...]) for slot, own in zip(far_slots, (own_a, own_b))]
        return jnp.concatenate(own, axis=1), jnp.concatenate([packed(far_a, j)[...], packed(far_b, j)[...]], axis=0), total[j]

    in_groups(
        list(range(rows)),
        load_far,
        lambda lhs, rhs, extra_t: (dot(lhs, rhs).T + extra_t).astype(BF16),
        square_t.__setitem__,
    )
    for at, send in enumerate((square_a, square_b)):
        for e in range(GX):
            send[e] = square_t[bases[at] + e]


def one_square(diag_own, x_t, diag_other):
    lhs = jnp.concatenate([diag_own, x_t], axis=1)
    rhs = jnp.concatenate([x_t, diag_other], axis=0)
    return dot(lhs, rhs).astype(BF16)


def finish(diag_own, x_t, square, diag_square_other):
    cube = dot(jnp.concatenate([diag_own, x_t], axis=1), jnp.concatenate([square, diag_square_other], axis=0))
    return (3.0 * square.astype(F32) - 2.0 * cube).astype(BF16)


def flipped(flag, block):
    return masked(flag, block).T


def inside_kernel(
    cols, own_a, own_b, diag_t, left_t, square_t, cube_in, diag_square_t, off_a, off_b,
    near_a, near_b, near_left, near_right,
    out, far_left, far_right, near_square, cube_t, local_out, near_other, sem,
):
    rows = diag_t.shape[0]
    edges = local_edges(rows)
    far_slots, _, bases = places(rows)
    copies = []
    for slot, place in ((2, 1), (4, 2), (1, 0), (5, 3)):
        own = [edge for edge in edges if edge[2] == place]
        first, last = (0, rows - 1) if abs(slot - CENTER) == 1 else (own[0][0], own[-1][0])

        def load(edge):
            j, _, _, k = edge
            return diag_t[j], left_t[place, j], square_t[place, j], diag_square_t[k]

        in_groups(own, load, finish, lambda edge, value: local_out.__setitem__((place, edge[0]), value))
        inside = [edge[0] for edge in own]
        for j in range(first, last + 1):
            if j not in inside:
                local_out[place, j] = jnp.zeros_like(diag_t[j])
        at = pl.ds(first, last + 1 - first)
        copies.append(pltpu.make_async_copy(local_out.at[place, at], out.at[at, slot], sem.at[place]))
        copies[-1].start()
    if rows != 2 * GX:
        cube_t[...] = cube_in[...]
    strip = list(range(GX))
    for side, near in enumerate((near_a, near_b)):
        base = bases[side]
        so_far = cube_in if rows == 2 * GX else cube_t
        in_groups(
            strip,
            lambda e: (diag_t[base + e], near_left[side, e], near[GX + e]),
            one_square,
            lambda e, value: near_square.__setitem__((side, e), value),
        )
        in_groups(
            strip,
            lambda e: (near[GX + e], near_right[side, e], diag_t[base + e]),
            one_square,
            lambda e, value: near_other.__setitem__((side, e), value),
        )
        in_groups(
            strip,
            lambda e: (near_left[side, e], near_other[side, e], so_far[base + e]),
            lambda x_t, square, extra: dot(x_t, square) + extra,
            lambda e, value: cube_t.__setitem__(base + e, value),
        )
    for at, (off, own) in enumerate(((off_a, own_a), (off_b, own_b))):
        slot = far_slots[at]
        in_groups(
            list(range(rows)),
            lambda j: (cols[slot, j] >= 0, packed(off, j)[...]),
            flipped,
            lambda j, value: far_left.__setitem__((at, j), value),
        )
        in_groups(
            list(range(rows)),
            lambda j: (cols[slot, j] >= 0, packed(own, j)[...]),
            flipped,
            lambda j, value: far_right.__setitem__((at, j), value),
        )
    for copy in copies:
        copy.wait()


def far_kernel(
    diag_t, cube_t, diag_square_t, far_left, far_right, diag_a, diag_b, old,
    out, far_part, far_square, far_other, diag_out, sem,
):
    rows = diag_t.shape[0]
    for at, diag in enumerate((diag_a, diag_b)):
        in_groups(
            list(range(rows)),
            lambda j: (diag_t[j], far_left[at, j], packed(diag, j)[...]),
            one_square,
            lambda j, value: far_square.__setitem__((at, j), value),
        )
        in_groups(
            list(range(rows)),
            lambda j: (diag_t[j], far_square[at, j]),
            lambda diag_own, square: 3.0 * square.astype(F32) - 2.0 * dot(diag_own, square),
            lambda j, value: far_part.__setitem__((at, j), value),
        )
        in_groups(
            list(range(rows)),
            lambda j: (packed(diag, j)[...], far_right[at, j], diag_t[j]),
            one_square,
            lambda j, value: far_other.__setitem__((at, j), value),
        )

    def load(j):
        lhs = jnp.concatenate([diag_t[j], far_left[0, j], far_left[1, j]], axis=1)
        rhs = jnp.concatenate([diag_square_t[j], far_other[0, j], far_other[1, j]], axis=0)
        return lhs, rhs, cube_t[j], diag_square_t[j]

    def last(lhs, rhs, extra, square):
        return (3.0 * square.astype(F32) - 2.0 * (dot(lhs, rhs) + extra)).astype(BF16)

    in_groups(list(range(rows)), load, last, diag_out.__setitem__)
    copy = pltpu.make_async_copy(diag_out, out.at[:, CENTER], sem)
    copy.start()
    copy.wait()


def near_last_kernel(diag_t, near_left, near_square, near_a, near_b, old, out, near_out, sem):
    _, near_slots, bases = places(diag_t.shape[0])
    copies = []
    for side, near in enumerate((near_a, near_b)):
        base = bases[side]
        in_groups(
            list(range(GX)),
            lambda e: (diag_t[base + e], near_left[side, e], near_square[side, e], near[e]),
            finish,
            lambda e, value: near_out.__setitem__((side, e), value),
        )
        target = out.at[pl.ds(base, GX), near_slots[side]]
        copies.append(pltpu.make_async_copy(near_out.at[side], target, sem.at[side]))
        copies[-1].start()
    for copy in copies:
        copy.wait()


def far_last_kernel(side, far_left, far_part, far, old, out, far_out, sem):
    rows = far.shape[0]
    slot = places(rows)[0][side]
    copies = []
    for part in range(rows // GX):
        first = part * GX
        in_groups(
            list(range(first, first + GX)),
            lambda j: (far_left[side, j], far[j], far_part[side, j]),
            lambda x_t, square, part: (part - 2.0 * dot(x_t, square)).astype(BF16),
            far_out.__setitem__,
        )
        at = pl.ds(first, GX)
        copies.append(pltpu.make_async_copy(far_out.at[at], out.at[at, slot], sem.at[part]))
        copies[-1].start()
    for copy in copies:
        copy.wait()


def on_device(density, block_cols):
    rows, _, size, _ = density.shape
    layer_dist = PLANE // rows
    count = lax.axis_size("row")

    def block(*dims):
        return jax.ShapeDtypeStruct((*dims, size, size), BF16)

    def wide(*dims):
        return jax.ShapeDtypeStruct((*dims, size, size), F32)

    def scratch(*dims):
        return pltpu.VMEM((*dims, size, size), BF16)

    cols = block_cols.T
    dma = pltpu.SemaphoreType.DMA
    smem = pl.BlockSpec(memory_space=pltpu.SMEM)
    vmem = pl.BlockSpec(memory_space=pltpu.VMEM)
    hbm = pl.BlockSpec(memory_space=pltpu.HBM)

    def call(kernel, in_specs, args, outs, out_specs, scratch_shapes, alias=None, vmem_limit=VMEM_LIMIT):
        return pl.pallas_call(
            kernel,
            in_specs=in_specs,
            out_specs=out_specs,
            out_shape=outs,
            scratch_shapes=scratch_shapes,
            input_output_aliases={} if alias is None else {alias: 0},
            compiler_params=pltpu.CompilerParams(vmem_limit_bytes=vmem_limit),
            cost_estimate=pl.CostEstimate(flops=0, bytes_accessed=KERNEL_COST, transcendentals=0),
        )(*args)

    def far(value, pairing):
        return lax.ppermute(value, "row", far_pairs(pairing, layer_dist, count))

    def near(value, pairing):
        return lax.ppermute(value, "row", near_pairs(pairing, layer_dist, count))

    rows_and_spare = jax.ShapeDtypeStruct((rows * size + SPARE, size), BF16)
    send_a, send_b = call(
        pack_kernel,
        [hbm],
        [density],
        [rows_and_spare] * 2,
        [vmem] * 2,
        [dma((2,))],
        vmem_limit=STAGE_LIMIT,
    )
    off_b = far(send_b, 1)
    off_a = far(send_a, 0)
    diag_t, diag_send, left_t, square_t, cube_t, total, strip_a, strip_b = call(
        local_kernel,
        [smem, vmem],
        [cols, density],
        [
            block(rows), rows_and_spare, block(4, rows), block(4, rows), wide(rows), wide(rows),
            block(2 * GX), block(2 * GX),
        ],
        [vmem] * 8,
        [],
    )
    diag_b = far(diag_send, 1)
    diag_a = far(diag_send, 0)
    near_b = near(strip_b, 1)
    near_a = near(strip_a, 0)
    diag_square_t, near_left, near_right, square_a, square_b = call(
        diag_square_kernel,
        [smem] + [vmem] * 9,
        [cols, strip_a, strip_b, send_a, send_b, total, near_a, near_b, off_a, off_b],
        [block(rows), block(2, GX), block(2, GX), block(GX), block(GX)],
        [vmem] * 5,
        [pltpu.VMEM((rows, size, size), F32)],
    )
    far_square_b = far(diag_square_t, 1)
    far_square_a = far(diag_square_t, 0)
    near_square_b = near(square_b, 1)
    near_square_a = near(square_a, 0)
    out, far_left, far_right, near_square, cube_t = call(
        inside_kernel,
        [smem] + [vmem] * 13,
        [
            cols, send_a, send_b, diag_t, left_t, square_t, cube_t, diag_square_t, off_a, off_b,
            near_a, near_b, near_left, near_right,
        ],
        [
            block(rows, K), block(2, rows), block(2, rows), block(2, GX), wide(rows),
        ],
        [hbm] + [vmem] * 4,
        [scratch(4, rows), scratch(2, GX), dma((4,))],
    )
    out = call(
        near_last_kernel,
        [vmem] * 5 + [hbm],
        [diag_t, near_left, near_square, near_square_a, near_square_b, out],
        block(rows, K),
        hbm,
        [scratch(2, GX), dma((2,))],
        alias=5,
    )
    out, far_part = call(
        far_kernel,
        [vmem] * 7 + [hbm],
        [diag_t, cube_t, diag_square_t, far_left, far_right, diag_a, diag_b, out],
        [block(rows, K), wide(2, rows)],
        [hbm, vmem],
        [scratch(2, rows), scratch(2, rows), scratch(rows), dma],
        alias=7,
    )
    for side, far_diag_square in ((0, far_square_a), (1, far_square_b)):
        out = call(
            functools.partial(far_last_kernel, side),
            [vmem] * 3 + [hbm],
            [far_left, far_part, far_diag_square, out],
            block(rows, K),
            hbm,
            [scratch(rows), dma((rows // GX,))],
            alias=3,
        )
    return out


def solution(mesh):
    placed = (P(("groups", "row"), None, None, None), P(("groups", "row"), None))
    return jax.shard_map(
        on_device,
        mesh=mesh,
        in_specs=placed,
        out_specs=P(("groups", "row"), None, None, None),
        check_vma=False,
    )
```
